32 devices in a mesh: dp: 8 (over y, x, core), tensor: 4 (over z).
Axes of the slice: x: 2, y: 2, z: 4, core: 2. Of those that a mesh axis runs over, the one named last changes fastest.
Arguments:
- inputs: float32 [2, 8, 2048, 512], P(None, 'dp', 'tensor'), may hold values from -6 to 6
- memory: float32 [2, 8, 256, 512], P(None, 'dp', 'tensor'), may hold values from -6 to 6
- lengths: int32 [2, 8, 13], P(None, 'dp'), may hold values from 32 to 1664, as said below
- parent: int32 [2, 8, 13], P(None, 'dp'), may hold values from 0 to 4, as said below
- self_qkv: float32 [3, 512, 512], P(None, 'dp', 'tensor'), may hold values from -0.25 to 0.25
- self_out: float32 [512, 512], P('tensor', 'dp'), may hold values from -1 to 1
- cross_q: float32 [512, 512], P('dp', 'tensor'), may hold values from -0.25 to 0.25
- cross_kv: float32 [2, 512, 512], P(None, 'dp', 'tensor'), may hold values from -0.25 to 0.25
- cross_out: float32 [512, 512], P('tensor', 'dp'), may hold values from -1 to 1
- ff_in: float32 [512, 2048], P('dp', 'tensor'), may hold values from -0.25 to 0.25
- ff_bias_in: float32 [2048], P('tensor'), may hold values from -3 to 3
- ff_out: float32 [2048, 512], P('tensor', 'dp'), may hold values from -0.125 to 0.125
- ff_bias_out: float32 [512], replicated, may hold values from -3 to 3
- cotangent: float32 [2, 8, 2048, 512], P(None, 'dp', 'tensor'), may hold values from -6 to 6
Outputs:
- output: float32 [2, 8, 2048, 512], P(None, 'dp', 'tensor')
- grad_inputs: float32 [2, 8, 2048, 512], P(None, 'dp', 'tensor')
- grad_memory: float32 [2, 8, 256, 512], P(None, 'dp', 'tensor')
- grad_self_qkv: float32 [3, 512, 512], P(None, 'dp', 'tensor')
- grad_self_out: float32 [512, 512], P('tensor', 'dp')
- grad_cross_q: float32 [512, 512], P('dp', 'tensor')
- grad_cross_kv: float32 [2, 512, 512], P(None, 'dp', 'tensor')
- grad_cross_out: float32 [512, 512], P('tensor', 'dp')
- grad_ff_in: float32 [512, 2048], P('dp', 'tensor')
- grad_ff_bias_in: float32 [2048], P('tensor')
- grad_ff_out: float32 [2048, 512], P('tensor', 'dp')
- grad_ff_bias_out: float32 [512], replicated
The draws below stay inside these ranges and needn't reach their ends.
Inputs may be any that keep to these rules, and one draw needn't show every extreme that they name: Each tree's 13 lengths sum to 2048; entry 0 is the trunk; entries 1 to 12 lie between 32 and 128, and one of them equals 32 in every tree; in some tree all of entries 1 to 12 equal 32. `parent`: entry 0 (the trunk) and entries 1 to 4 (the branches) are 0; entries 5 to 12 (the leaves) each name a branch, 1 to 4, and every branch is named by some leaf.
All inputs are finite; a program needn't handle non-finite values.
Results may differ from the reference program's by a relative error of at most 0.0003.
Values sent between devices are 32-bit elements; how exact they have to be, the bound alone decides.
No kernel may reach another device: no remote copies, remote signals or barrier semaphores. Data moves between devices by JAX's collectives and lax.ppermute only.
A program may use at most 384 MiB of HBM per device.

```python
import jax
import jax.numpy as jnp
from jax import lax

D = 512
FF = 2048
HEADS = 8
HEAD = 64
TREE_LEN = 2048
MEM = 256
SEGS = 13
MICRO = 2
TREES = 8
SEG_MOST = 128
SEG_LEAST = 32


def draw_one_lengths(key):
    first_key, second_key = jax.random.split(key)
    others = jax.random.randint(first_key, (SEGS - 1,), SEG_LEAST, SEG_MOST + 1, dtype=jnp.int32)
    chosen = jax.random.randint(second_key, (), 0, SEGS - 1, dtype=jnp.int32)
    others = jnp.where(jnp.arange(SEGS - 1, dtype=jnp.int32) == chosen, SEG_LEAST, others).astype(jnp.int32)
    trunk_len = (TREE_LEN - jnp.sum(others)).astype(jnp.int32)
    return jnp.concatenate([trunk_len[None], others]).astype(jnp.int32)


def draw_lengths(key, part):
    tree_keys = jax.random.split(jax.random.fold_in(key, 11), MICRO * TREES)
    drawn = jax.vmap(draw_one_lengths)(tree_keys)
    widest = jax.random.randint(jax.random.fold_in(key, 37), (), 0, MICRO * TREES, dtype=jnp.int32)
    shortest = jnp.full((SEGS - 1,), SEG_LEAST, jnp.int32)
    trunk_most = jnp.full((1,), TREE_LEN - (SEGS - 1) * SEG_LEAST, jnp.int32)
    extreme = jnp.concatenate([trunk_most, shortest]).astype(jnp.int32)
    picked = (jnp.arange(MICRO * TREES, dtype=jnp.int32) == widest)[:, None]
    drawn = jnp.where(picked, extreme[None, :], drawn).astype(jnp.int32)
    return drawn.reshape(MICRO, TREES, SEGS)


def draw_one_parent(key):
    first_key, second_key = jax.random.split(key)
    covering = (jax.random.permutation(first_key, 4) + 1).astype(jnp.int32)
    additional = jax.random.randint(second_key, (4,), 1, 5, dtype=jnp.int32)
    return jnp.concatenate([jnp.zeros((5,), jnp.int32), covering, additional]).astype(jnp.int32)


def draw_parent(key, part):
    tree_keys = jax.random.split(jax.random.fold_in(key, 23), MICRO * TREES)
    return jax.vmap(draw_one_parent)(tree_keys).reshape(MICRO, TREES, SEGS)


def block_levels(stream_key, extent, pieces, least, high):
    def one(position, shards_of):
        heights = jax.random.uniform(jax.random.fold_in(jax.random.fold_in(stream_key, 6), position), (shards_of,), jnp.float32, least / len(pieces), high / len(pieces))
        return jnp.repeat(jnp.exp(heights), extent[position] // shards_of).reshape((-1,) + (1,) * (len(extent) - position - 1))

    gain = one(*pieces[0])
    for cut in pieces[1:]:
        gain = gain * one(*cut)
    return gain


def centred(stream_key, shape, spread, limit, pieces=(), kind=jnp.bfloat16):
    entries = spread * jax.random.normal(stream_key, shape, jnp.float32)
    if pieces:
        entries = entries * block_levels(stream_key, shape, pieces, -0.22, 0.18)
    return jnp.clip(entries, -limit, limit).astype(kind)


def setup_inputs(seed: int = 0) -> dict:
    key_list = jax.random.split(jax.random.key(seed), 15)
    inputs = centred(key_list[0], (MICRO, TREES, TREE_LEN, D), 1.0, 6.0, ((1, 8), (2, 4)), jnp.float32)
    memory = centred(key_list[1], (MICRO, TREES, MEM, D), 1.0, 6.0, ((1, 8), (2, 4)), jnp.float32)
    lengths = draw_lengths(jax.random.fold_in(key_list[14], 71), 0)
    parent = draw_parent(jax.random.fold_in(key_list[14], 71), 0)
    self_qkv = centred(key_list[4], (3, D, D), D ** -0.5, 0.25, ((1, 8), (2, 4)), jnp.float32)
    self_out = centred(key_list[5], (D, D), (D // 16) ** -0.5, 1.0, ((0, 4), (1, 8)), jnp.float32)
    cross_q = centred(key_list[6], (D, D), D ** -0.5, 0.25, ((0, 8), (1, 4)), jnp.float32)
    cross_kv = centred(key_list[7], (2, D, D), D ** -0.5, 0.25, ((1, 8), (2, 4)), jnp.float32)
    cross_out = centred(key_list[8], (D, D), (D // 16) ** -0.5, 1.0, ((0, 4), (1, 8)), jnp.float32)
    ff_in = centred(key_list[9], (D, FF), D ** -0.5, 0.25, ((0, 8), (1, 4)), jnp.float32)
    ff_bias_in = centred(key_list[10], (FF,), 0.5, 3.0, ((0, 4),), jnp.float32)
    ff_out = centred(key_list[11], (FF, D), FF ** -0.5, 0.125, ((0, 4), (1, 8)), jnp.float32)
    ff_bias_out = centred(key_list[12], (D,), 0.5, 3.0, (), jnp.float32)
    cotangent = centred(key_list[13], (MICRO, TREES, TREE_LEN, D), 1.0, 6.0, ((1, 8), (2, 4)), jnp.float32)
    return {"inputs": inputs, "memory": memory, "lengths": lengths, "parent": parent, "self_qkv": self_qkv, "self_out": self_out, "cross_q": cross_q, "cross_kv": cross_kv, "cross_out": cross_out, "ff_in": ff_in, "ff_bias_in": ff_bias_in, "ff_out": ff_out, "ff_bias_out": ff_bias_out, "cotangent": cotangent}


HIGH = lax.Precision.HIGHEST
NEG = -1e+30

@jax.custom_vjp
def low(v):
    return lax.optimization_barrier(v.astype(jnp.bfloat16)).astype(jnp.float32)

@jax.custom_vjp
def low_back(v):
    return v

def low_keep(v):
    return (low(v), None)

def low_pass(kept, grad):
    return (grad,)

def back_keep(v):
    return (v, None)

def back_low(kept, grad):
    return (low(grad),)
low.defvjp(low_keep, low_pass)
low_back.defvjp(back_keep, back_low)

def product(left, right):
    return jnp.dot(left, right, precision=HIGH)

def tree_paths(tree_lengths, tree_parent):
    ends = jnp.cumsum(tree_lengths).astype(jnp.int32)
    places = jnp.arange(TREE_LEN, dtype=jnp.int32)
    segment = lax.optimization_barrier(jnp.sum((places[:, None] >= ends[None, :-1]).astype(jnp.int32), axis=1)).astype(jnp.int32)
    labels = jnp.arange(SEGS, dtype=jnp.int32)
    first_up = lax.optimization_barrier(jnp.sum(jnp.where(segment[:, None] == labels[None, :], tree_parent[None, :], 0), axis=1)).astype(jnp.int32)
    second_up = lax.optimization_barrier(jnp.sum(jnp.where(first_up[:, None] == labels[None, :], tree_parent[None, :], 0), axis=1)).astype(jnp.int32)
    return (segment, first_up, second_up)

def allowed(path_info, first_row, block_rows):
    segment, first_up, second_up = path_info
    row_seg = lax.dynamic_slice_in_dim(segment, first_row, block_rows)
    row_first = lax.dynamic_slice_in_dim(first_up, first_row, block_rows)
    row_second = lax.dynamic_slice_in_dim(second_up, first_row, block_rows)
    row_place = first_row + jnp.arange(block_rows, dtype=jnp.int32)
    key_place = jnp.arange(TREE_LEN, dtype=jnp.int32)
    same_seg = (row_seg[:, None] == segment[None, :]) & (row_place[:, None] >= key_place[None, :])
    ancestor = (row_seg[:, None] > 0) & ((segment[None, :] == row_first[:, None]) | (segment[None, :] == row_second[:, None]))
    return same_seg | ancestor

def attention(queries, keys, values, path_info):
    row_count = queries.shape[0]
    block_rows = min(512, row_count)
    scale = HEAD ** (-0.5)
    key_heads = keys.reshape(keys.shape[0], HEADS, HEAD)
    value_heads = values.reshape(values.shape[0], HEADS, HEAD)

    def one_block(first_row):
        rows = lax.dynamic_slice_in_dim(queries, first_row, block_rows, 0).reshape(block_rows, HEADS, HEAD)
        scores = jnp.einsum('qhe,khe->hqk', rows, key_heads, precision=HIGH) * scale
        if path_info is not None:
            scores = jnp.where(allowed(path_info, first_row, block_rows)[None], scores, NEG)
        probs = jax.nn.softmax(scores, axis=-1)
        return jnp.einsum('hqk,khe->qhe', probs, value_heads, precision=HIGH).reshape(block_rows, D)
    starts = jnp.arange(row_count // block_rows, dtype=jnp.int32) * block_rows
    return lax.map(jax.checkpoint(one_block), starts).reshape(row_count, D)

def decoder_layer(tokens, memory_rows, params, path_info):
    qkv_w, attn_w, cross_qw, cross_kvw, cross_ow, in_w, bias_in, out_w, bias_out = params
    attn = attention(product(tokens, qkv_w[0]), product(tokens, qkv_w[1]), product(tokens, qkv_w[2]), path_info)
    hidden_one = tokens + product(attn, attn_w)
    context = attention(product(hidden_one, cross_qw), product(memory_rows, cross_kvw[0]), product(memory_rows, cross_kvw[1]), None)
    hidden_two = hidden_one + product(context, cross_ow)
    pre_act = product(hidden_two, in_w) + bias_in
    return hidden_two + product(jax.nn.gelu(pre_act, approximate=False), out_w) + bias_out

def reference(inputs, memory, lengths, parent, self_qkv, self_out, cross_q, cross_kv, cross_out, ff_in, ff_bias_in, ff_out, ff_bias_out, cotangent):
    tree_count = MICRO * TREES
    weights = (self_qkv, self_out, cross_q, cross_kv, cross_out, ff_in, ff_bias_in, ff_out, ff_bias_out)
    stacked = (inputs.reshape(tree_count, TREE_LEN, D), memory.reshape(tree_count, MEM, D), cotangent.reshape(tree_count, TREE_LEN, D), lengths.reshape(tree_count, SEGS), parent.reshape(tree_count, SEGS))

    def one_tree(totals, tree_item):
        tokens, memory_rows, grad_rows, tree_lengths, tree_parent = tree_item
        path_info = tree_paths(tree_lengths, tree_parent)

        def forward(tok_arg, mem_arg, params):
            return decoder_layer(tok_arg, mem_arg, params, path_info)
        output_rows, pullback = jax.vjp(forward, tokens, memory_rows, weights)
        grad_tokens, grad_mem, grad_params = pullback(grad_rows)
        return (jax.tree.map(jnp.add, totals, grad_params), (output_rows, grad_tokens, grad_mem))
    zero_grads = jax.tree.map(jnp.zeros_like, weights)
    totals, (outputs, grad_tokens, grad_mem) = lax.scan(one_tree, zero_grads, stacked)
    return (outputs.reshape(MICRO, TREES, TREE_LEN, D), grad_tokens.reshape(MICRO, TREES, TREE_LEN, D), grad_mem.reshape(MICRO, TREES, MEM, D), totals[0], totals[1], totals[2], totals[3], totals[4], totals[5], totals[6], totals[7], totals[8])
```

```python
import functools

import jax
import jax.numpy as jnp
from jax import lax
from jax.experimental import pallas as pl
from jax.experimental.pallas import tpu as pltpu
from jax.sharding import PartitionSpec as P

HEAD = 64
LOG2E = 1.4426950408889634
LN2 = 0.6931471805599453
BF = jnp.bfloat16
F32 = jnp.float32
NT = (((1,), (1,)), ((), ()))
NN = (((1,), (0,)), ((), ()))


def dot(a, b, dims=NN):
    return lax.dot_general(a, b, dims, preferred_element_type=F32)


def split(x):
    hi = x.astype(BF).astype(F32)
    return hi, x - hi


def attn_fwd_kernel(q_ref, k_ref, v_ref, qa_ref, ka_ref, o_ref, l_ref, qs, ks, vt, *, causal, qb, kb, rq, rk):
    lane = lax.broadcasted_iota(jnp.int32, (256, 128), 1)
    left = lane < HEAD

    def sel(a, b):
        return jnp.where(left, a, b)

    def build_q(i, _):
        r = pl.ds(pl.multiple_of(i * 256, 256), 256)
        x = q_ref[r, :] * (HEAD ** -0.5 * LOG2E)
        hi, lo = split(x)
        hir, lor = pltpu.roll(hi, HEAD, 1), pltpu.roll(lo, HEAD, 1)
        aux = qa_ref[r, :].astype(F32) if causal else jnp.zeros((256, 128), F32)
        qs[0, r, 0:128] = sel(hi, hir).astype(BF)
        qs[0, r, 128:256] = sel(lo, aux).astype(BF)
        qs[1, r, 0:128] = sel(hir, hi).astype(BF)
        qs[1, r, 128:256] = sel(lor, aux).astype(BF)
        return 0

    def build_k(i, _):
        r = pl.ds(pl.multiple_of(i * 256, 256), 256)
        hi, lo = split(k_ref[r, :])
        hir, lor = pltpu.roll(hi, HEAD, 1), pltpu.roll(lo, HEAD, 1)
        aux = ka_ref[r, :].astype(F32) if causal else jnp.zeros((256, 128), F32)
        ks[0, r, 0:128] = sel(hi, lor).astype(BF)
        ks[0, r, 128:256] = sel(hi, aux).astype(BF)
        ks[1, r, 0:128] = sel(hir, lo).astype(BF)
        ks[1, r, 128:256] = sel(hir, aux).astype(BF)
        hi, lo = split(v_ref[r, :])
        hir, lor = pltpu.roll(hi, HEAD, 1), pltpu.roll(lo, HEAD, 1)
        vt[0, :, r] = sel(hi, lor).T.astype(BF)
        vt[1, :, r] = sel(hir, lo).T.astype(BF)
        return 0

    lax.fori_loop(0, rq // 256, build_q, 0)
    lax.fori_loop(0, rk // 256, build_k, 0)

    def one_q(i, _):
        rows = pl.ds(pl.multiple_of(i * qb, qb), qb)
        qh = [qs[h, rows, :] for h in range(2)]

        def step(carry, first_key, diag):
            keys = pl.ds(pl.multiple_of(first_key, kb), kb)
            out = []
            for h in range(2):
                m, s, acc = carry[h]
                st = dot(ks[h, keys, :], qh[h], NT)
                if diag:
                    kk = lax.broadcasted_iota(jnp.int32, (kb, qb), 0)
                    qq = lax.broadcasted_iota(jnp.int32, (kb, qb), 1)
                    st = jnp.where(kk <= qq, st, -1e30)
                mn = jnp.maximum(m, jnp.max(st, axis=0, keepdims=True))
                p = jnp.exp2(st - mn)
                al = jnp.exp2(m - mn)
                s = s * al + jnp.sum(p, axis=0, keepdims=True)
                ph = p.astype(BF)
                plo = (p - ph.astype(F32)).astype(BF)
                acc = acc * al + dot(vt[h, :, keys], ph) + dot(vt[h, :, keys], plo)
                out.append((mn, s, acc))
            return tuple(out)

        init = (jnp.full((1, qb), -1e30, F32), jnp.zeros((1, qb), F32), jnp.zeros((128, qb), F32))
        carry = (init, init)
        if causal:
            carry = lax.fori_loop(0, i * (qb // kb), lambda j, c: step(c, j * kb, False), carry)
            assert qb == kb
            carry = step(carry, i * qb, True)
        else:
            for j in range(rk // kb):
                carry = step(carry, j * kb, False)
        outs = []
        for h in range(2):
            m, s, acc = carry[h]
            outs.append((acc[0:HEAD] + acc[HEAD:]) / s)
            l_ref[0, h:h + 1, rows] = m + jnp.log2(s)
        o_ref[rows, :] = jnp.concatenate(outs, axis=0).T
        return 0

    lax.fori_loop(0, rq // qb, one_q, 0)


def attn_fwd(q, k, v, qaux, kaux, causal, qb=256, kb=256):
    rq, w = q.shape
    rk = k.shape[0]
    pairs = w // 128
    ra = qaux.shape[0]
    qspec = pl.BlockSpec((rq, 128), lambda p: (0, p))
    kspec = pl.BlockSpec((rk, 128), lambda p: (0, p))
    return pl.pallas_call(
        functools.partial(attn_fwd_kernel, causal=causal, qb=qb, kb=kb, rq=rq, rk=rk),
        grid=(pairs,),
        in_specs=[qspec, kspec, kspec,
                  pl.BlockSpec((ra, 128), lambda p: (0, 0)), pl.BlockSpec((ra, 128), lambda p: (0, 0))],
        out_specs=[qspec, pl.BlockSpec((1, 2, rq), lambda p: (p, 0, 0))],
        out_shape=[jax.ShapeDtypeStruct((rq, w), F32), jax.ShapeDtypeStruct((pairs, 2, rq), F32)],
        scratch_shapes=[pltpu.VMEM((2, rq, 256), BF), pltpu.VMEM((2, rk, 256), BF), pltpu.VMEM((2, 128, rk), BF)],
        compiler_params=pltpu.CompilerParams(vmem_limit_bytes=48 << 20),
        cost_estimate=pl.CostEstimate(flops=int(2e9) * pairs, bytes_accessed=rq * w * 16, transcendentals=0),
        name="attn_fwd",
    )(q, k, v, qaux, kaux)


def attn_bwd_kernel(q_ref, k_ref, v_ref, do_ref, l_ref, d_ref, qa_ref, ka_ref, dq_ref, dk_ref, dv_ref,
                    qs, ks, kt, vs, dos, dka, dva, *, causal, qb, kb, rq, rk):
    lane = lax.broadcasted_iota(jnp.int32, (256, 128), 1)
    left = lane < HEAD

    def sel(a, b):
        return jnp.where(left, a, b)

    def build_q(i, _):
        r = pl.ds(pl.multiple_of(i * 256, 256), 256)
        hi, lo = split(q_ref[r, :] * (HEAD ** -0.5 * LOG2E))
        hir, lor = pltpu.roll(hi, HEAD, 1), pltpu.roll(lo, HEAD, 1)
        aux = qa_ref[r, :].astype(F32) if causal else jnp.zeros((256, 128), F32)
        qs[0, r, 0:128] = sel(hi, lor).astype(BF)
        qs[0, r, 128:256] = sel(hi, aux).astype(BF)
        qs[1, r, 0:128] = sel(hir, lo).astype(BF)
        qs[1, r, 128:256] = sel(hir, aux).astype(BF)
        hi, lo = split(do_ref[r, :])
        hir, lor = pltpu.roll(hi, HEAD, 1), pltpu.roll(lo, HEAD, 1)
        zero = jnp.zeros((256, 128), F32)
        dos[0, r, 0:128] = sel(hi, lor).astype(BF)
        dos[0, r, 128:256] = sel(hi, zero).astype(BF)
        dos[1, r, 0:128] = sel(hir, lo).astype(BF)
        dos[1, r, 128:256] = sel(hir, zero).astype(BF)
        return 0

    def build_k(i, _):
        r = pl.ds(pl.multiple_of(i * 256, 256), 256)
        hi, lo = split(k_ref[r, :])
        hir, lor = pltpu.roll(hi, HEAD, 1), pltpu.roll(lo, HEAD, 1)
        aux = ka_ref[r, :].astype(F32) if causal else jnp.zeros((256, 128), F32)
        ks[0, r, 0:128] = sel(hi, hir).astype(BF)
        ks[0, r, 128:256] = sel(lo, aux).astype(BF)
        ks[1, r, 0:128] = sel(hir, hi).astype(BF)
        ks[1, r, 128:256] = sel(lor, aux).astype(BF)
        kt[0, :, r] = sel(hi, lor).T.astype(BF)
        kt[1, :, r] = sel(hir, lo).T.astype(BF)
        hi, lo = split(v_ref[r, :])
        hir, lor = pltpu.roll(hi, HEAD, 1), pltpu.roll(lo, HEAD, 1)
        zero = jnp.zeros((256, 128), F32)
        vs[0, r, 0:128] = sel(hi, hir).astype(BF)
        vs[0, r, 128:256] = sel(lo, zero).astype(BF)
        vs[1, r, 0:128] = sel(hir, hi).astype(BF)
        vs[1, r, 128:256] = sel(lor, zero).astype(BF)
        dka[0, r, :] = zero
        dka[1, r, :] = zero
        dva[0, r, :] = zero
        dva[1, r, :] = zero
        return 0

    lax.fori_loop(0, rq // 256, build_q, 0)
    lax.fori_loop(0, rk // 256, build_k, 0)

    def one_q(i, _):
        rows = pl.ds(pl.multiple_of(i * qb, qb), qb)

        def step(carry, first_key, diag):
            keys = pl.ds(pl.multiple_of(first_key, kb), kb)
            out = []
            for h in range(2):
                acc = carry[h]
                qh = qs[h, rows, :]
                dh = dos[h, rows, :]
                st = dot(ks[h, keys, :], qh, NT)
                if diag:
                    kk = lax.broadcasted_iota(jnp.int32, (kb, qb), 0)
                    qq = lax.broadcasted_iota(jnp.int32, (kb, qb), 1)
                    st = jnp.where(kk <= qq, st, -1e30)
                p = jnp.exp2(st - l_ref[0, h:h + 1, rows])
                ph = p.astype(BF)
                plo = (p - ph.astype(F32)).astype(BF)
                dhl = dh[:, 0:128]
                dva[h, keys, :] += dot(ph, dhl) + dot(plo, dhl)
                dp = dot(vs[h, keys, :], dh, NT)
                ds = p * (dp - d_ref[0, h:h + 1, rows])
                dsh = ds.astype(BF)
                dsl = (ds - dsh.astype(F32)).astype(BF)
                qhl = qh[:, 0:128]
                dka[h, keys, :] += dot(dsh, qhl) + dot(dsl, qhl)
                kth = kt[h, :, keys]
                acc = acc + dot(kth, dsh) + dot(kth, dsl)
                out.append(acc)
            return tuple(out)

        init = jnp.zeros((128, qb), F32)
        carry = (init, init)
        if causal:
            carry = lax.fori_loop(0, i * (qb // kb), lambda j, c: step(c, j * kb, False), carry)
            carry = step(carry, i * qb, True)
        else:
            for j in range(rk // kb):
                carry = step(carry, j * kb, False)
        outs = [(a[0:HEAD] + a[HEAD:]) * (HEAD ** -0.5) for a in carry]
        dq_ref[rows, :] = jnp.concatenate(outs, axis=0).T
        return 0

    lax.fori_loop(0, rq // qb, one_q, 0)

    def finish(i, _):
        r = pl.ds(pl.multiple_of(i * 256, 256), 256)
        a, b = dka[0, r, :], dka[1, r, :]
        dk_ref[r, :] = sel(a + pltpu.roll(a, HEAD, 1), b + pltpu.roll(b, HEAD, 1)) * LN2
        a, b = dva[0, r, :], dva[1, r, :]
        dv_ref[r, :] = sel(a + pltpu.roll(a, HEAD, 1), b + pltpu.roll(b, HEAD, 1))
        return 0

    lax.fori_loop(0, rk // 256, finish, 0)


def attn_bwd(q, k, v, do, lse, delta, qaux, kaux, causal, qb=256, kb=256):
    rq, w = q.shape
    rk = k.shape[0]
    pairs = w // 128
    ra = qaux.shape[0]
    qspec = pl.BlockSpec((rq, 128), lambda p: (0, p))
    kspec = pl.BlockSpec((rk, 128), lambda p: (0, p))
    lspec = pl.BlockSpec((1, 2, rq), lambda p: (p, 0, 0))
    aspec = pl.BlockSpec((ra, 128), lambda p: (0, 0))
    return pl.pallas_call(
        functools.partial(attn_bwd_kernel, causal=causal, qb=qb, kb=kb, rq=rq, rk=rk),
        grid=(pairs,),
        in_specs=[qspec, kspec, kspec, qspec, lspec, lspec, aspec, aspec],
        out_specs=[qspec, kspec, kspec],
        out_shape=[jax.ShapeDtypeStruct((rq, w), F32), jax.ShapeDtypeStruct((rk, w), F32), jax.ShapeDtypeStruct((rk, w), F32)],
        scratch_shapes=[pltpu.VMEM((2, rq, 256), BF), pltpu.VMEM((2, rk, 256), BF), pltpu.VMEM((2, 128, rk), BF),
                        pltpu.VMEM((2, rk, 256), BF), pltpu.VMEM((2, rq, 256), BF),
                        pltpu.VMEM((2, rk, 128), F32), pltpu.VMEM((2, rk, 128), F32)],
        compiler_params=pltpu.CompilerParams(vmem_limit_bytes=56 << 20),
        cost_estimate=pl.CostEstimate(flops=int(5e9) * pairs, bytes_accessed=rq * w * 32, transcendentals=0),
        name="attn_bwd",
    )(q, k, v, do, lse, delta, qaux, kaux)


def tree_aux(lengths, parent, n):
    segs = lengths.shape[0]
    ends = jnp.cumsum(lengths)
    places = jnp.arange(n, dtype=jnp.int32)
    seg = jnp.sum((places[:, None] >= ends[None, :-1]).astype(jnp.int32), axis=1)
    labels = jnp.arange(segs, dtype=jnp.int32)
    onehot = seg[:, None] == labels[None, :]
    up1 = jnp.sum(jnp.where(onehot, parent[None, :], 0), axis=1)
    up2 = jnp.sum(jnp.where(up1[:, None] == labels[None, :], parent[None, :], 0), axis=1)
    lab = jnp.arange(128, dtype=jnp.int32)[None, :] - HEAD
    inside = (lab >= 0) & (lab < segs)
    sg = seg[:, None]
    kaux = jnp.where(inside & (lab == sg), 1.0, 0.0).astype(BF)
    ok = (lab == sg) | ((sg > 0) & ((lab == up1[:, None]) | (lab == up2[:, None])))
    qaux = jnp.where(inside & ~ok, -1e30, 0.0).astype(BF)
    return qaux, kaux


HIGH = lax.Precision.HIGH
TN = (((0,), (0,)), ((), ()))
ROOT_HALF = 0.7071067811865476
NORMAL_PEAK = 0.3989422804014327
BOTH = ("dp", "tensor")


def mm(a, b, dims=NN):
    return lax.dot_general(a, b, dims, precision=HIGH, preferred_element_type=F32)


def flip_bit(size, bit):
    return [(i, i ^ (1 << bit)) for i in range(size)]


def item_routes(dp, tensor):
    routes = []
    for turn in range(2):
        pairs = []
        for c in range(dp // 2):
            for t in range(2):
                for z in range(tensor):
                    b = (z + turn) % 2
                    pairs.append(((2 * c + t) * tensor + z, (2 * c + z // 2) * tensor + 2 * b + t))
        routes.append(pairs)
    return routes


def scatter_items(x, routes, z):
    first = lax.ppermute(lax.dynamic_index_in_dim(x, z % 2, 0, keepdims=False), BOTH, routes[0])
    second = lax.ppermute(lax.dynamic_index_in_dim(x, 1 - z % 2, 0, keepdims=False), BOTH, routes[1])
    even = z // 2 == 0
    return jnp.where(even, jnp.concatenate([first, second]), jnp.concatenate([second, first]))


def return_items(rows, routes, z):
    half = rows.shape[0] // 2
    b = z // 2
    back = [[(d, s) for s, d in r] for r in routes]
    first = lax.ppermute(lax.dynamic_slice_in_dim(rows, b * half, half), BOTH, back[0])
    second = lax.ppermute(lax.dynamic_slice_in_dim(rows, (1 - b) * half, half), BOTH, back[1])
    even = z % 2 == 0
    return jnp.where(even, jnp.stack([first, second]), jnp.stack([second, first]))


def swap(x, dp):
    return lax.ppermute(x, "dp", flip_bit(dp, 0))


def both_cores(mine, other, k):
    return jnp.where(k == 0, jnp.concatenate([mine, other]), jnp.concatenate([other, mine]))


def flip_where(x, axis, flag):
    return jnp.where(flag, lax.rev(x, (axis,)), x)


def gather_weights(x, dp, tensor, d, z):
    bits = dp.bit_length() - 1
    parts = [x] + [
        lax.ppermute(x, "tensor", [(i, (i + s) % tensor) for i in range(tensor)]) for s in range(1, tensor)
    ]
    around = jnp.stack(parts)
    order = (z - jnp.arange(tensor)) % tensor
    rows = x.shape[0]
    halves = []
    for part, seq in ((0, list(range(1, bits))), (1, list(range(bits - 1, 0, -1)))):
        cur = around[None, :, part * rows // 2:(part + 1) * rows // 2]
        rel = [0]
        for bit in seq + [0]:
            cur = jnp.concatenate([cur, lax.ppermute(cur, "dp", flip_bit(dp, bit))])
            rel = rel + [r ^ (1 << bit) for r in rel]
        place = jnp.argsort(jnp.array(rel))
        halves.append((cur, place))
    return halves, order


def place_kernel(ta_ref, tb_ref, ts_ref, a_ref, b_ref, *outs, widths):
    half = a_ref.shape[2]
    start = 0
    for o, w in zip(outs, widths):
        o[0:half, :] = a_ref[0, 0, :, start:start + w]
        o[half:, :] = b_ref[0, 0, :, start:start + w]
        start += w


def full_weights(x, widths, dp, tensor, d, z):
    rows = x.shape[0]
    if rows % 16:
        g = lax.all_gather(x, BOTH, axis=0).reshape(dp, tensor, rows, x.shape[1])
        outs, start = [], 0
        for w in widths:
            outs.append(g[:, :, :, start:start + w].transpose(0, 2, 1, 3).reshape(dp * rows, tensor * w))
            start += w
        return outs
    ((a, pa), (b, pb)), _ = gather_weights(x, dp, tensor, d, z)
    who = jnp.arange(dp)
    ta, tb = pa[who ^ d].astype(jnp.int32), pb[who ^ d].astype(jnp.int32)
    ts = ((z - jnp.arange(tensor)) % tensor).astype(jnp.int32)
    total = x.shape[1]
    return pl.pallas_call(
        functools.partial(place_kernel, widths=widths),
        grid_spec=pltpu.PrefetchScalarGridSpec(
            num_scalar_prefetch=3,
            grid=(dp, tensor),
            in_specs=[
                pl.BlockSpec((1, 1, rows // 2, total), lambda i, j, ta, tb, ts: (ta[i], ts[j], 0, 0)),
                pl.BlockSpec((1, 1, rows // 2, total), lambda i, j, ta, tb, ts: (tb[i], ts[j], 0, 0)),
            ],
            out_specs=[pl.BlockSpec((rows, w), lambda i, j, ta, tb, ts: (i, j)) for w in widths],
        ),
        out_shape=[jax.ShapeDtypeStruct((dp * rows, tensor * w), F32) for w in widths],
        cost_estimate=pl.CostEstimate(flops=0, bytes_accessed=8 * dp * tensor * rows * total, transcendentals=0),
        name="place_weights",
    )(ta, tb, ts, a, b)


def pick(x, axis, index):
    return lax.dynamic_index_in_dim(x, index, axis, keepdims=False)


def pack_grads(mats, dp, tensor):
    parts = []
    for m in mats:
        r, w = m.shape[0] // dp, m.shape[1] // tensor
        parts.append(m.reshape(dp, r, tensor, w).transpose(0, 2, 1, 3))
    return jnp.concatenate(parts, axis=3)


def sum_columns(part, dp, tensor, d, z):
    bits = dp.bit_length() - 1
    rows, width = part.shape[2:]
    halves = []
    for which, seq in ((0, list(range(1, bits))), (1, list(range(bits - 1, 0, -1)))):
        cur = part[:, :, which * rows // 2:(which + 1) * rows // 2]
        left = sorted(range(1, bits), reverse=True)
        cur = cur.reshape((2,) * len(left) + cur.shape[1:])
        for bit in seq:
            axis = left.index(bit)
            mine = (d >> bit) & 1
            sent = lax.ppermute(pick(cur, axis, 1 - mine), "dp", flip_bit(dp, bit))
            cur = pick(cur, axis, mine) + sent
            left.remove(bit)
        halves.append(cur)
    cur = jnp.concatenate(halves, axis=1)
    total = pick(cur, 0, z)
    for s in range(1, tensor):
        total = total + lax.ppermute(
            pick(cur, 0, (z + s) % tensor), "tensor", [(i, (i + s) % tensor) for i in range(tensor)]
        )
    return total


def reduce_grads(mats, dp, tensor, d, z):
    part = pack_grads(mats, dp, tensor)
    if part.shape[2] % 16:
        flat = part.reshape((dp * tensor,) + part.shape[2:])
        return lax.psum_scatter(flat, BOTH, scatter_dimension=0, tiled=False)
    part = part.reshape((dp // 2, 2) + part.shape[1:])
    mine = pick(part, 1, d % 2) + swap(pick(part, 1, 1 - d % 2), dp)
    return sum_columns(mine, dp, tensor, d, z)


def reduce_head_grads(mats, dp, tensor, d, z):
    part = pack_grads(mats, dp, tensor // 2)
    k = d % 2
    if part.shape[2] % 16:
        none = jnp.zeros_like(part)
        full = jnp.where(k == 0, jnp.concatenate([part, none], 1), jnp.concatenate([none, part], 1))
        flat = full.reshape((dp * tensor,) + part.shape[2:])
        return lax.psum_scatter(flat, BOTH, scatter_dimension=0, tiled=False)
    part = part.reshape((dp // 2, 2) + part.shape[1:])
    mine, other = pick(part, 1, k), swap(pick(part, 1, 1 - k), dp)
    joined = jnp.where(k == 0, jnp.concatenate([mine, other], 1), jnp.concatenate([other, mine], 1))
    return sum_columns(joined, dp, tensor, d, z)


def on_device(
    inputs, memory, lengths, parent, self_qkv, self_out, cross_q, cross_kv, cross_out,
    ff_in, ff_bias_in, ff_out, ff_bias_out, cotangent,
):
    dp, tensor = lax.axis_size("dp"), lax.axis_size("tensor")
    d, z = lax.axis_index("dp"), lax.axis_index("tensor")
    k = d % 2
    routes = item_routes(dp, tensor)
    rows = inputs.shape[2] * 2
    width = inputs.shape[3]
    heads_wide = width // 2
    hw = self_qkv.shape[2]

    x = scatter_items(inputs[:, 0], routes, z)
    x_all = both_cores(x, swap(x, dp), k)
    qkv_w = full_weights(
        jnp.concatenate([self_qkv[0], self_qkv[1], self_qkv[2]], axis=1), [hw] * 3, dp, tensor, d, z
    )
    own_w = [lax.dynamic_slice_in_dim(w, k * heads_wide, heads_wide, 1) for w in qkv_w]
    out_t, cq, ck, cv, cross_out_t = full_weights(
        jnp.concatenate([self_out.T, cross_q, cross_kv[0], cross_kv[1], cross_out.T], axis=1),
        [hw] * 5, dp, tensor, d, z,
    )
    mem = scatter_items(memory[:, 0], routes, z)
    mem_all = both_cores(mem, swap(mem, dp), k)
    w_in, w_out_t = full_weights(jnp.concatenate([ff_in, ff_out.T], axis=1), [ff_in.shape[1]] * 2, dp, tensor, d, z)
    bias_in = lax.all_gather(ff_bias_in, "tensor", axis=0, tiled=True)
    g = scatter_items(cotangent[:, 0], routes, z)

    other_len, other_par = swap(lengths, dp), swap(parent, dp)
    tree = z % 2
    my_len = jnp.where(tree == k, lengths[:, 0], other_len[:, 0])[z // 2]
    my_par = jnp.where(tree == k, parent[:, 0], other_par[:, 0])[z // 2]
    qaux, kaux = tree_aux(my_len, my_par, 2 * rows)

    q, key, val = (mm(x_all, w) for w in own_w)
    attn, lse = attn_fwd(q, key, val, qaux, kaux, True)
    mine = lax.dynamic_slice_in_dim(attn, k * rows, rows)
    other = swap(lax.dynamic_slice_in_dim(attn, (1 - k) * rows, rows), dp)
    attn_rows = jnp.where(k == 0, jnp.concatenate([mine, other], 1), jnp.concatenate([other, mine], 1))

    h1 = x + mm(attn_rows, out_t, NT)
    q2 = mm(h1, cq)
    k2, v2 = mm(mem_all, ck), mm(mem_all, cv)
    ctx, lse2 = attn_fwd(q2, k2, v2, qaux, kaux, False)
    h2 = h1 + mm(ctx, cross_out_t, NT)
    u = mm(h2, w_in) + bias_in
    cdf = 0.5 * (1.0 + lax.erf(u * ROOT_HALF))
    act = u * cdf
    output = h2 + mm(act, w_out_t, NT) + ff_bias_out
    du = mm(g, w_out_t) * (cdf + u * NORMAL_PEAK * jnp.exp(-0.5 * u * u))
    grad_out_t = mm(g, act, TN)
    grad_in = mm(h2, du, TN)
    grad_bias = jnp.concatenate([jnp.sum(du, axis=0), jnp.sum(g, axis=0)])
    dh2 = g + mm(du, w_in, NT)
    dctx = mm(dh2, cross_out_t)
    grad_cross_out_t = mm(dh2, ctx, TN)
    heads = width // HEAD
    pick_heads = (jnp.arange(width)[None, :] // HEAD == jnp.arange(heads)[:, None]).astype(F32)

    def deltas(a, b):
        prod = a * b
        n = prod.shape[1] // HEAD
        return lax.dot_general(
            pick_heads[:n, :prod.shape[1]], prod, NT, precision=lax.Precision.HIGHEST
        ).reshape(n // 2, 2, prod.shape[0])

    dq2, dk2, dv2 = attn_bwd(q2, k2, v2, dctx, lse2, deltas(dctx, ctx), qaux, kaux, False)
    grad_cross_q = mm(h1, dq2, TN)
    grad_ck, grad_cv = mm(mem_all, dk2, TN), mm(mem_all, dv2, TN)
    mem_part = mm(dk2, ck, NT) + mm(dv2, cv, NT)
    mem_rows = mem_part.shape[0] // 2
    grad_mem = lax.dynamic_slice_in_dim(mem_part, k * mem_rows, mem_rows) + swap(
        lax.dynamic_slice_in_dim(mem_part, (1 - k) * mem_rows, mem_rows), dp
    )
    dh1 = dh2 + mm(dq2, cq, NT)
    dattn_rows = mm(dh1, out_t)
    grad_self_out_t = mm(dh1, attn_rows, TN)
    mine = lax.dynamic_slice_in_dim(dattn_rows, k * heads_wide, heads_wide, 1)
    other = swap(lax.dynamic_slice_in_dim(dattn_rows, (1 - k) * heads_wide, heads_wide, 1), dp)
    dattn = both_cores(mine, other, k)
    dq, dk, dv = attn_bwd(q, key, val, dattn, lse, deltas(dattn, attn), qaux, kaux, True)
    part = mm(dq, own_w[0], NT) + mm(dk, own_w[1], NT) + mm(dv, own_w[2], NT)
    dx = (
        dh1
        + lax.dynamic_slice_in_dim(part, k * rows, rows)
        + swap(lax.dynamic_slice_in_dim(part, (1 - k) * rows, rows), dp)
    )
    grad_qkv = [mm(x_all, t, TN) for t in (dq, dk, dv)]

    ff = reduce_grads([grad_in, grad_out_t], dp, tensor, d, z)
    mid = reduce_grads([grad_self_out_t, grad_cross_q, grad_ck, grad_cv, grad_cross_out_t], dp, tensor, d, z)
    att = reduce_head_grads(grad_qkv, dp, tensor, d, z)
    grad_bias = lax.psum(grad_bias, BOTH)
    fw = ff_in.shape[1]
    out_rows = return_items(output, routes, z)
    grad_x = return_items(dx, routes, z)
    grad_m = return_items(grad_mem, routes, z)
    return (
        out_rows[:, None],
        grad_x[:, None],
        grad_m[:, None],
        jnp.stack([att[:, i * hw:(i + 1) * hw] for i in range(3)]),
        mid[:, 0:hw].T,
        mid[:, hw:2 * hw],
        jnp.stack([mid[:, 2 * hw:3 * hw], mid[:, 3 * hw:4 * hw]]),
        mid[:, 4 * hw:5 * hw].T,
        ff[:, :fw],
        lax.dynamic_slice_in_dim(grad_bias, z * fw, fw),
        ff[:, fw:].T,
        grad_bias[tensor * fw:],
    )


def solution(mesh):
    rows4 = P(None, "dp", "tensor", None)
    col3, row2, col2 = P(None, "dp", "tensor"), P("tensor", "dp"), P("dp", "tensor")
    idx = P(None, "dp", None)
    return jax.shard_map(
        on_device,
        mesh=mesh,
        in_specs=(rows4, rows4, idx, idx, col3, row2, col2, col3, row2, col2, P("tensor"), row2, P(), rows4),
        out_specs=(rows4, rows4, rows4, col3, row2, col2, col3, row2, col2, P("tensor"), row2, P()),
        check_vma=False,
    )
```

```python
import functools

import jax
import jax.numpy as jnp
from jax import lax
from jax.experimental import pallas as pl
from jax.experimental.pallas import tpu as pltpu
from jax.sharding import PartitionSpec as P

HEAD = 64
LOG2E = 1.4426950408889634
LN2 = 0.6931471805599453
BF = jnp.bfloat16
F32 = jnp.float32
NT = (((1,), (1,)), ((), ()))
NN = (((1,), (0,)), ((), ()))


def dot(a, b, dims=NN):
    return lax.dot_general(a, b, dims, preferred_element_type=F32)


def split(x):
    hi = x.astype(BF).astype(F32)
    return hi, x - hi


def attn_fwd_kernel(q_ref, k_ref, v_ref, qa_ref, ka_ref, *refs, causal, qb, kb, rq, rk):
    o_ref, l_ref, qs, ks, vt = refs[-5:]
    lane = lax.broadcasted_iota(jnp.int32, (256, 128), 1)
    left = lane < HEAD

    def sel(a, b):
        return jnp.where(left, a, b)

    def build_q(i, _):
        r = pl.ds(pl.multiple_of(i * 256, 256), 256)
        x = q_ref[r, :] * (HEAD ** -0.5 * LOG2E)
        hi, lo = split(x)
        hir, lor = pltpu.roll(hi, HEAD, 1), pltpu.roll(lo, HEAD, 1)
        aux = qa_ref[r, :].astype(F32) if causal else jnp.zeros((256, 128), F32)
        qs[0, r, 0:128] = sel(hi, hir).astype(BF)
        qs[0, r, 128:256] = sel(lo, aux).astype(BF)
        qs[1, r, 0:128] = sel(hir, hi).astype(BF)
        qs[1, r, 128:256] = sel(lor, aux).astype(BF)
        return 0

    def build_k(i, _):
        r = pl.ds(pl.multiple_of(i * 256, 256), 256)
        hi, lo = split(k_ref[r, :])
        hir, lor = pltpu.roll(hi, HEAD, 1), pltpu.roll(lo, HEAD, 1)
        aux = ka_ref[r, :].astype(F32) if causal else jnp.zeros((256, 128), F32)
        ks[0, r, 0:128] = sel(hi, lor).astype(BF)
        ks[0, r, 128:256] = sel(hi, aux).astype(BF)
        ks[1, r, 0:128] = sel(hir, lo).astype(BF)
        ks[1, r, 128:256] = sel(hir, aux).astype(BF)
        hi, lo = split(v_ref[r, :])
        hir, lor = pltpu.roll(hi, HEAD, 1), pltpu.roll(lo, HEAD, 1)
        vt[0, :, r] = sel(hi, lor).T.astype(BF)
        vt[1, :, r] = sel(hir, lo).T.astype(BF)
        return 0

    lax.fori_loop(0, rq // 256, build_q, 0)
    lax.fori_loop(0, rk // 256, build_k, 0)

    def one_q(i, _):
        rows = pl.ds(pl.multiple_of(i * qb, qb), qb)

        def update(state, qh, h, keys, mask):
            m, s, acc = state
            st = dot(ks[h, keys, :], qh, NT)
            if mask is not None:
                kk = lax.broadcasted_iota(jnp.int32, st.shape, 0)
                qq = lax.broadcasted_iota(jnp.int32, st.shape, 1)
                st = jnp.where(kk - qq <= mask, st, -1e30)
            mn = jnp.maximum(m, jnp.max(st, axis=0, keepdims=True))
            p = jnp.exp2(st - mn)
            al = jnp.exp2(m - mn)
            s = s * al + jnp.sum(p, axis=0, keepdims=True)
            ph = p.astype(BF)
            plo = (p - ph.astype(F32)).astype(BF)
            return mn, s, acc * al + dot(vt[h, :, keys], ph) + dot(vt[h, :, keys], plo)

        qh = [qs[h, rows, :] for h in range(2)]

        def step(j, carry):
            keys = pl.ds(pl.multiple_of(j * kb, kb), kb)
            return tuple(update(carry[h], qh[h], h, keys, None) for h in range(2))

        init = (jnp.full((1, qb), -1e30, F32), jnp.zeros((1, qb), F32), jnp.zeros((128, qb), F32))
        carry = (init, init)
        if causal:
            carry = lax.fori_loop(0, i * qb // kb, step, carry)
            sub = qb // 2
            for j in range(2):
                keys = pl.ds(pl.multiple_of(i * qb + j * sub, sub), sub)
                new = []
                for h in range(2):
                    part = tuple(t[:, j * sub:] for t in carry[h])
                    part = update(part, qh[h][j * sub:], h, keys, 0)
                    if j:
                        part = tuple(jnp.concatenate([t[:, :sub], u], axis=1) for t, u in zip(carry[h], part))
                    new.append(part)
                carry = tuple(new)
        else:
            for j in range(rk // kb):
                carry = step(j, carry)
        outs = []
        for h in range(2):
            m, s, acc = carry[h]
            outs.append((acc[0:HEAD] + acc[HEAD:]) / s)
            l_ref[0, h:h + 1, rows] = m + jnp.log2(s)
        o_ref[rows, :] = jnp.concatenate(outs, axis=0).T
        return 0

    lax.fori_loop(0, rq // qb, one_q, 0)


def attn_fwd(q, k, v, qaux, kaux, causal, qb=512, kb=512, deps=()):
    rq, w = q.shape
    rk = k.shape[0]
    pairs = w // 128
    ra = qaux.shape[0]
    qspec = pl.BlockSpec((rq, 128), lambda p: (0, p))
    kspec = pl.BlockSpec((rk, 128), lambda p: (0, p))
    return pl.pallas_call(
        functools.partial(attn_fwd_kernel, causal=causal, qb=qb, kb=kb, rq=rq, rk=rk),
        grid=(pairs,),
        in_specs=[qspec, kspec, kspec,
                  pl.BlockSpec((ra, 128), lambda p: (0, 0)), pl.BlockSpec((ra, 128), lambda p: (0, 0))]
        + [pl.BlockSpec(memory_space=pl.ANY)] * len(deps),
        out_specs=[qspec, pl.BlockSpec((1, 2, rq), lambda p: (p, 0, 0))],
        out_shape=[jax.ShapeDtypeStruct((rq, w), F32), jax.ShapeDtypeStruct((pairs, 2, rq), F32)],
        scratch_shapes=[pltpu.VMEM((2, rq, 256), BF), pltpu.VMEM((2, rk, 256), BF), pltpu.VMEM((2, 128, rk), BF)],
        compiler_params=pltpu.CompilerParams(vmem_limit_bytes=32 << 20),
        cost_estimate=pl.CostEstimate(flops=(int(2e10) if causal else int(4e9)) * pairs, bytes_accessed=rq * w * 16, transcendentals=0),
        name="attn_fwd",
    )(q, k, v, qaux, kaux, *deps)


def attn_bwd_kernel(q_ref, k_ref, v_ref, do_ref, l_ref, d_ref, qa_ref, ka_ref, *refs, causal, qb, kb, rq, rk):
    dq_ref, dk_ref, dv_ref, qs, ks, kt, vs, dos, dka, dva = refs[-10:]
    lane = lax.broadcasted_iota(jnp.int32, (256, 128), 1)
    left = lane < HEAD

    def sel(a, b):
        return jnp.where(left, a, b)

    def build_q(i, _):
        r = pl.ds(pl.multiple_of(i * 256, 256), 256)
        hi, lo = split(q_ref[r, :] * (HEAD ** -0.5 * LOG2E))
        hir, lor = pltpu.roll(hi, HEAD, 1), pltpu.roll(lo, HEAD, 1)
        aux = qa_ref[r, :].astype(F32) if causal else jnp.zeros((256, 128), F32)
        qs[0, r, 0:128] = sel(hi, lor).astype(BF)
        qs[0, r, 128:256] = sel(hi, aux).astype(BF)
        qs[1, r, 0:128] = sel(hir, lo).astype(BF)
        qs[1, r, 128:256] = sel(hir, aux).astype(BF)
        hi, lo = split(do_ref[r, :])
        hir, lor = pltpu.roll(hi, HEAD, 1), pltpu.roll(lo, HEAD, 1)
        zero = jnp.zeros((256, 128), F32)
        dos[0, r, 0:128] = sel(hi, lor).astype(BF)
        dos[0, r, 128:256] = sel(hi, zero).astype(BF)
        dos[1, r, 0:128] = sel(hir, lo).astype(BF)
        dos[1, r, 128:256] = sel(hir, zero).astype(BF)
        return 0

    def build_k(i, _):
        r = pl.ds(pl.multiple_of(i * 256, 256), 256)
        hi, lo = split(k_ref[r, :])
        hir, lor = pltpu.roll(hi, HEAD, 1), pltpu.roll(lo, HEAD, 1)
        aux = ka_ref[r, :].astype(F32) if causal else jnp.zeros((256, 128), F32)
        ks[0, r, 0:128] = sel(hi, hir).astype(BF)
        ks[0, r, 128:256] = sel(lo, aux).astype(BF)
        ks[1, r, 0:128] = sel(hir, hi).astype(BF)
        ks[1, r, 128:256] = sel(lor, aux).astype(BF)
        kt[0, :, r] = sel(hi, lor).T.astype(BF)
        kt[1, :, r] = sel(hir, lo).T.astype(BF)
        hi, lo = split(v_ref[r, :])
        hir, lor = pltpu.roll(hi, HEAD, 1), pltpu.roll(lo, HEAD, 1)
        zero = jnp.zeros((256, 128), F32)
        vs[0, r, 0:128] = sel(hi, hir).astype(BF)
        vs[0, r, 128:256] = sel(lo, zero).astype(BF)
        vs[1, r, 0:128] = sel(hir, hi).astype(BF)
        vs[1, r, 128:256] = sel(lor, zero).astype(BF)
        dka[0, r, :] = zero
        dka[1, r, :] = zero
        dva[0, r, :] = zero
        dva[1, r, :] = zero
        return 0

    lax.fori_loop(0, rq // 256, build_q, 0)
    lax.fori_loop(0, rk // 256, build_k, 0)

    def one_q(i, _):
        rows = pl.ds(pl.multiple_of(i * qb, qb), qb)

        def update(acc, h, keys, cols, mask):
            qh = qs[h, cols, :]
            dh = dos[h, cols, :]
            st = dot(ks[h, keys, :], qh, NT)
            if mask is not None:
                kk = lax.broadcasted_iota(jnp.int32, st.shape, 0)
                qq = lax.broadcasted_iota(jnp.int32, st.shape, 1)
                st = jnp.where(kk - qq <= mask, st, -1e30)
            p = jnp.exp2(st - l_ref[0, h:h + 1, cols])
            ph = p.astype(BF)
            plo = (p - ph.astype(F32)).astype(BF)
            dhl = dh[:, 0:128]
            dva[h, keys, :] += dot(ph, dhl) + dot(plo, dhl)
            dp = dot(vs[h, keys, :], dh, NT)
            ds = p * (dp - d_ref[0, h:h + 1, cols])
            dsh = ds.astype(BF)
            dsl = (ds - dsh.astype(F32)).astype(BF)
            qhl = qh[:, 0:128]
            dka[h, keys, :] += dot(dsh, qhl) + dot(dsl, qhl)
            kth = kt[h, :, keys]
            return acc + dot(kth, dsh) + dot(kth, dsl)

        def step(j, carry):
            keys = pl.ds(pl.multiple_of(j * kb, kb), kb)
            return tuple(update(carry[h], h, keys, rows, None) for h in range(2))

        init = jnp.zeros((128, qb), F32)
        carry = (init, init)
        if causal:
            carry = lax.fori_loop(0, i * qb // kb, step, carry)
            sub = qb // 2
            for j in range(2):
                keys = pl.ds(pl.multiple_of(i * qb + j * sub, sub), sub)
                cols = pl.ds(pl.multiple_of(i * qb + j * sub, sub), qb - j * sub)
                new = []
                for h in range(2):
                    part = update(carry[h][:, j * sub:], h, keys, cols, 0)
                    if j:
                        part = jnp.concatenate([carry[h][:, :sub], part], axis=1)
                    new.append(part)
                carry = tuple(new)
        else:
            for j in range(rk // kb):
                carry = step(j, carry)
        outs = [(a[0:HEAD] + a[HEAD:]) * (HEAD ** -0.5) for a in carry]
        dq_ref[rows, :] = jnp.concatenate(outs, axis=0).T
        return 0

    lax.fori_loop(0, rq // qb, one_q, 0)

    def finish(i, _):
        r = pl.ds(pl.multiple_of(i * 256, 256), 256)
        a, b = dka[0, r, :], dka[1, r, :]
        dk_ref[r, :] = sel(a + pltpu.roll(a, HEAD, 1), b + pltpu.roll(b, HEAD, 1)) * LN2
        a, b = dva[0, r, :], dva[1, r, :]
        dv_ref[r, :] = sel(a + pltpu.roll(a, HEAD, 1), b + pltpu.roll(b, HEAD, 1))
        return 0

    lax.fori_loop(0, rk // 256, finish, 0)


def attn_bwd(q, k, v, do, lse, delta, qaux, kaux, causal, qb=512, kb=512, pair=None, deps=()):
    rq, w = q.shape
    rk = k.shape[0]
    pairs = 1 if pair is not None else w // 128
    first = pair or 0
    ra = qaux.shape[0]
    qspec = pl.BlockSpec((rq, 128), lambda p: (0, p + first))
    kspec = pl.BlockSpec((rk, 128), lambda p: (0, p + first))
    lspec = pl.BlockSpec((1, 2, rq), lambda p: (p + first, 0, 0))
    aspec = pl.BlockSpec((ra, 128), lambda p: (0, 0))
    return pl.pallas_call(
        functools.partial(attn_bwd_kernel, causal=causal, qb=qb, kb=kb, rq=rq, rk=rk),
        grid=(pairs,),
        in_specs=[qspec, kspec, kspec, qspec, lspec, lspec, aspec, aspec]
        + [pl.BlockSpec(memory_space=pl.ANY)] * len(deps),
        out_specs=[pl.BlockSpec((n, 128), lambda p: (0, p)) for n in (rq, rk, rk)],
        out_shape=[jax.ShapeDtypeStruct((n, pairs * 128), F32) for n in (rq, rk, rk)],
        scratch_shapes=[pltpu.VMEM((2, rq, 256), BF), pltpu.VMEM((2, rk, 256), BF), pltpu.VMEM((2, 128, rk), BF),
                        pltpu.VMEM((2, rk, 256), BF), pltpu.VMEM((2, rq, 256), BF),
                        pltpu.VMEM((2, rk, 128), F32), pltpu.VMEM((2, rk, 128), F32)],
        compiler_params=pltpu.CompilerParams(vmem_limit_bytes=40 << 20),
        cost_estimate=pl.CostEstimate(flops=(int(3.4e10) if causal else int(5e9)) * pairs, bytes_accessed=rq * w * 32, transcendentals=0),
        name="attn_bwd",
    )(q, k, v, do, lse, delta, qaux, kaux, *deps)


def tree_aux(lengths, parent, n):
    segs = lengths.shape[0]
    ends = jnp.cumsum(lengths)
    places = jnp.arange(n, dtype=jnp.int32)
    seg = jnp.sum((places[:, None] >= ends[None, :-1]).astype(jnp.int32), axis=1)
    labels = jnp.arange(segs, dtype=jnp.int32)
    onehot = seg[:, None] == labels[None, :]
    up1 = jnp.sum(jnp.where(onehot, parent[None, :], 0), axis=1)
    up2 = jnp.sum(jnp.where(up1[:, None] == labels[None, :], parent[None, :], 0), axis=1)
    lab = jnp.arange(128, dtype=jnp.int32)[None, :] - HEAD
    inside = (lab >= 0) & (lab < segs)
    sg = seg[:, None]
    kaux = jnp.where(inside & (lab == sg), 1.0, 0.0).astype(BF)
    ok = (lab == sg) | ((sg > 0) & ((lab == up1[:, None]) | (lab == up2[:, None])))
    qaux = jnp.where(inside & ~ok, -1e30, 0.0).astype(BF)
    return qaux, kaux


HIGH = lax.Precision.HIGH
TN = (((0,), (0,)), ((), ()))
BOTH = ("dp", "tensor")
ANY = pl.BlockSpec(memory_space=pl.ANY)
VMEM = pl.BlockSpec(memory_space=pltpu.VMEM)
SMEM = pl.BlockSpec(memory_space=pltpu.SMEM)


def mm(a, b, dims=NN):
    return lax.dot_general(a, b, dims, precision=HIGH, preferred_element_type=F32)


def nothing(*refs):
    pass


def after(x, *others):
    return pl.pallas_call(
        nothing,
        in_specs=[ANY] * (1 + len(others)),
        out_specs=ANY,
        out_shape=jax.ShapeDtypeStruct(x.shape, x.dtype),
        input_output_aliases={0: 0},
        name="after",
    )(x, *others)


def flip_bit(size, bit):
    return [(i, i ^ (1 << bit)) for i in range(size)]


def turn(size, by):
    return [(i, (i + by) % size) for i in range(size)]


def pick(x, axis, index):
    return lax.dynamic_index_in_dim(x, index, axis, keepdims=False)


def item_routes(dp, tensor):
    routes = []
    for step in range(2):
        pairs = []
        for c in range(dp // 2):
            for t in range(2):
                for z in range(tensor):
                    b = (z + step) % 2
                    pairs.append(((2 * c + t) * tensor + z, (2 * c + z // 2) * tensor + 2 * b + t))
        routes.append(pairs)
    return routes


def send_items(x, routes, z, *others):
    first, second = pick(x, 0, z % 2), pick(x, 0, 1 - z % 2)
    if others:
        first, second = after(first, *others), after(second, *others)
    return lax.ppermute(first, BOTH, routes[0]), lax.ppermute(second, BOTH, routes[1])


def in_order(first, second, z):
    return jnp.where(z // 2 == 0, jnp.concatenate([first, second]), jnp.concatenate([second, first]))


def return_items(rows, routes, z):
    half = rows.shape[0] // 2
    b = z // 2
    back = [[(t, s) for s, t in r] for r in routes]
    first = lax.ppermute(lax.dynamic_slice_in_dim(rows, b * half, half), BOTH, back[0])
    second = lax.ppermute(lax.dynamic_slice_in_dim(rows, (1 - b) * half, half), BOTH, back[1])
    return first, second


def both_batches(first, second, z):
    return jnp.where(z % 2 == 0, jnp.stack([first, second]), jnp.stack([second, first]))


def swap(x, dp):
    return lax.ppermute(x, "dp", flip_bit(dp, 0))


def both_cores(mine, other, k, axis=0):
    return jnp.where(
        k == 0, jnp.concatenate([mine, other], axis), jnp.concatenate([other, mine], axis)
    )


def rows_kernel(who_ref, a_ref, b_ref, c_ref, d_ref, o_ref):
    k, m = who_ref[0], who_ref[1]
    half = a_ref.shape[0]
    for ref, core, which in ((a_ref, k, m), (b_ref, k, 1 - m), (c_ref, 1 - k, m), (d_ref, 1 - k, 1 - m)):
        o_ref[pl.ds(pl.multiple_of((2 * core + which) * half, half), half), :] = ref[...]


def place_rows(first, second, other_first, other_second, k, z):
    half, width = first.shape
    who = jnp.stack([k, z // 2]).astype(jnp.int32)
    return pl.pallas_call(
        rows_kernel,
        in_specs=[SMEM, VMEM, VMEM, VMEM, VMEM],
        out_specs=VMEM,
        out_shape=jax.ShapeDtypeStruct((4 * half, width), F32),
        compiler_params=pltpu.CompilerParams(vmem_limit_bytes=32 << 20),
        cost_estimate=pl.CostEstimate(flops=0, bytes_accessed=32 * half * width, transcendentals=0),
        name="place_rows",
    )(who, first, second, other_first, other_second)


ROOT_HALF = 0.7071067811865476
NORMAL_PEAK = 0.3989422804014327


def parts2(x):
    hi = x.astype(BF)
    return hi, (x - hi.astype(F32)).astype(BF)


def dot3(a, b, dims=NN):
    return dot(a[0], b[0], dims) + (dot(a[0], b[1], dims) + dot(a[1], b[0], dims))


def ffn_kernel(z_ref, h_ref, g_ref, wi_ref, wo_ref, bo_ref, out_ref, dh_ref, gr_ref,
               hh, hl, gh, gl, hth, htl, gth, gtl, ah, al, dh, dl, *, rb, drows):
    j = pl.program_id(0)
    n = h_ref.shape[0]

    @pl.when(j == 0)
    def _():
        for r in range(n // rb):
            rows = slice(r * rb, (r + 1) * rb)
            for ref, h, l, th, tl in ((h_ref, hh, hl, hth, htl), (g_ref, gh, gl, gth, gtl)):
                x = ref[rows, :]
                h[rows, :], l[rows, :] = parts2(x)
                th[:, rows], tl[:, rows] = parts2(x.T)
            out_ref[rows, :] = h_ref[rows, :] + bo_ref[0:1, :]
            dh_ref[rows, :] = g_ref[rows, :]

    dp = wi_ref.shape[0]
    wide = wi_ref.shape[3]
    wi = parts2(wi_ref[:, 0, 0:drows, :].reshape(dp * drows, wide))
    wo = parts2(wo_ref[:, 0, 0:drows, :].reshape(dp * drows, wide))
    bias = wi_ref[0, 0, drows:drows + 1, :]
    total = jnp.zeros((1, wide), F32)
    for r in range(n // rb):
        rows = slice(r * rb, (r + 1) * rb)
        u = dot3((hh[rows, :], hl[rows, :]), wi) + bias
        gz = dot3((gh[rows, :], gl[rows, :]), wo)
        cdf = 0.5 * (1.0 + lax.erf(u * ROOT_HALF))
        act = u * cdf
        du = gz * (cdf + u * (NORMAL_PEAK * jnp.exp(-0.5 * u * u)))
        total = total + jnp.sum(du, axis=0, keepdims=True)
        act, du = parts2(act), parts2(du)
        ah[rows, :], al[rows, :] = act
        dh[rows, :], dl[rows, :] = du
        out_ref[rows, :] += dot3(act, wo, NT)
        dh_ref[rows, :] += dot3(du, wi, NT)
    gr_ref[:, 0:drows, 0:wide] = dot3((hth[...], htl[...]), (dh[...], dl[...])).reshape(dp, drows, wide)
    gr_ref[:, 0:drows, wide:] = dot3((gth[...], gtl[...]), (ah[...], al[...])).reshape(dp, drows, wide)
    gr_ref[:, drows:drows + 8, :] = jnp.zeros((dp, 8, 2 * wide), F32)
    for i in range(dp):
        gr_ref[i, drows:drows + 1, 0:wide] = total

    for half in range(2):
        @pl.when(j % 2 == half)
        def _():
            bout = jnp.sum(g_ref[:, half * wide:(half + 1) * wide], axis=0, keepdims=True)
            for i in range(dp):
                gr_ref[i, drows + 1:drows + 2, 0:wide] = bout


def ffn(h2, g, ff_all, bias_out, z, drows):
    n, width = h2.shape
    dp, tensor, high, both = ff_all.shape
    wide = both // 4
    steps = 2 * tensor
    full = lambda: pl.BlockSpec((n, width), lambda j, z: (0, 0))
    return pl.pallas_call(
        functools.partial(ffn_kernel, rb=512, drows=drows),
        grid_spec=pltpu.PrefetchScalarGridSpec(
            num_scalar_prefetch=1,
            grid=(steps,),
            in_specs=[
                full(), full(),
                pl.BlockSpec((dp, 1, high, wide), lambda j, z: (0, (z[0] + tensor - j // 2) % tensor, 0, j % 2)),
                pl.BlockSpec((dp, 1, high, wide), lambda j, z: (0, (z[0] + tensor - j // 2) % tensor, 0, 2 + j % 2)),
                pl.BlockSpec((1, width), lambda j, z: (0, 0)),
            ],
            out_specs=[full(), full(), pl.BlockSpec((dp, high, 2 * wide), lambda j, z: (0, 0, j))],
            scratch_shapes=[pltpu.VMEM((n, width), BF)] * 4 + [pltpu.VMEM((width, n), BF)] * 4
            + [pltpu.VMEM((n, wide), BF)] * 4,
        ),
        out_shape=[
            jax.ShapeDtypeStruct((n, width), F32),
            jax.ShapeDtypeStruct((n, width), F32),
            jax.ShapeDtypeStruct((dp, high, 2 * wide * steps), F32),
        ],
        compiler_params=pltpu.CompilerParams(vmem_limit_bytes=48 << 20),
        cost_estimate=pl.CostEstimate(flops=int(5e10), bytes_accessed=30 << 20, transcendentals=0),
        name="ffn",
    )(z[None].astype(jnp.int32), h2, g, ff_all, ff_all, bias_out[None])


def around(x, tensor):
    return [x] + [lax.ppermute(x, "tensor", turn(tensor, s)) for s in range(1, tensor)]


def place_kernel(who_ref, g_ref, *outs, widths, own):
    k, z = who_ref[0], who_ref[1]
    tensor = g_ref.shape[1]
    half = tensor // 2
    for s in range(tensor):
        col = (z + tensor - s) % tensor
        start = 0
        for o, w, only in zip(outs, widths, own):
            def copy(c, o=o, w=w, s=s, start=start):
                o[:, pl.ds(pl.multiple_of(c * w, w), w)] = g_ref[0, s, :, start:start + w]

            if only:
                pl.when(col // half == k)(functools.partial(copy, col % half))
            else:
                copy(col)
            start += w


def place_weights(g, widths, own, k, z):
    dp, tensor, rows, wide = g.shape
    who = jnp.stack([k, z]).astype(jnp.int32)
    cols = [w * (tensor // 2 if o else tensor) for o, w in zip(own, widths)]
    return pl.pallas_call(
        functools.partial(place_kernel, widths=widths, own=own),
        grid=(dp,),
        in_specs=[SMEM, pl.BlockSpec((1, tensor, rows, wide), lambda i: (i, 0, 0, 0))],
        out_specs=[pl.BlockSpec((rows, c), lambda i: (i, 0)) for c in cols],
        out_shape=[jax.ShapeDtypeStruct((dp * rows, c), F32) for c in cols],
        cost_estimate=pl.CostEstimate(flops=0, bytes_accessed=8 * dp * tensor * rows * wide, transcendentals=0),
        name="place_weights",
    )(who, g)


def halve(cur, seq, dp, d):
    left = sorted(seq, reverse=True)
    cur = cur.reshape((2,) * len(left) + cur.shape[1:])
    for bit in seq:
        axis = left.index(bit)
        mine = (d >> bit) & 1
        sent = lax.ppermute(pick(cur, axis, 1 - mine), "dp", flip_bit(dp, bit))
        cur = pick(cur, axis, mine) + sent
        left.remove(bit)
    return cur


def along_z(parts, tensor, z):
    total = parts(z)
    for s in range(1, tensor):
        total = total + lax.ppermute(parts((z + s) % tensor), "tensor", turn(tensor, s))
    return total


def column_block(x, i, tensor):
    w = x.shape[-1] // tensor
    return lax.dynamic_slice_in_dim(x, i * w, w, x.ndim - 1)


def reduce_over_dp(mats, dp, tensor, earlier):
    whole = jnp.concatenate([m.reshape(dp, m.shape[0] // dp, m.shape[1]) for m in mats], axis=2)
    mine = lax.psum_scatter(after(whole, earlier), "dp", scatter_dimension=0, tiled=False)
    blocks, start = [], 0
    for i in range(tensor):
        one, start = [], 0
        for m in mats:
            w = m.shape[1] // tensor
            one.append(mine[:, start + i * w:start + (i + 1) * w])
            start += m.shape[1]
        blocks.append(jnp.concatenate(one, axis=1))
    return jnp.stack(blocks)


def reduce_over_tensor(blocks, widths):
    total = lax.psum_scatter(blocks, "tensor", scatter_dimension=0, tiled=False)
    outs, start = [], 0
    for w in widths:
        outs.append(total[:, start:start + w])
        start += w
    return outs


def reduce_head_grads(mats, dp, tensor, d, z):
    bits = dp.bit_length() - 1
    k = d % 2
    half = tensor // 2
    rows = mats[0].shape[0] // dp
    w = mats[0].shape[1] // half
    split = [m.reshape(dp // 2, 2, rows, half, w) for m in mats]

    def side(i, u):
        return jnp.concatenate([pick(m, 1, i)[:, :, u] for m in split], axis=2)

    chains = []
    for u in range(half):
        seq = list(range(1, bits))
        if u % 2:
            seq = seq[::-1]
        both = jnp.stack([side(k, u), swap(side(1 - k, u), dp)], axis=1)
        chains.append(halve(both, seq, dp, d))
    everything = jnp.stack(chains)

    def parts(i):
        return pick(pick(everything, 0, i % half), 0, (i // half + k) % 2)

    total = along_z(parts, tensor, z)
    return [total[:, i * w:(i + 1) * w] for i in range(len(mats))]


def on_device(
    inputs, memory, lengths, parent, self_qkv, self_out, cross_q, cross_kv, cross_out,
    ff_in, ff_bias_in, ff_out, ff_bias_out, cotangent,
):
    dp, tensor = lax.axis_size("dp"), lax.axis_size("tensor")
    d, z = lax.axis_index("dp"), lax.axis_index("tensor")
    k = d % 2
    routes = item_routes(dp, tensor)
    rows = inputs.shape[2] * 2
    width = inputs.shape[3]
    heads_wide = width // 2
    hw = self_qkv.shape[2]
    fw = ff_in.shape[1]
    drows = ff_in.shape[0]

    shard = jnp.concatenate(
        [self_qkv[0], self_qkv[1], self_qkv[2], self_out.T, cross_q, cross_kv[0], cross_kv[1], cross_out.T], axis=1
    )
    parts = around(shard, tensor)
    x1, x2 = send_items(inputs[:, 0], routes, z, *parts[1:])
    weights = lax.all_gather(jnp.stack(parts), "dp", axis=0)
    wq, wk, wv, out_t, cq, ck, cv, cross_out_t = place_weights(
        weights, [hw] * 8, [True] * 3 + [False] * 5, k, z
    )
    own_w = [wq, wk, wv]

    bias_rows = jnp.concatenate([ff_bias_in[None], jnp.zeros((7, fw), F32)])
    ff_shard = jnp.concatenate(
        [jnp.concatenate([ff_in, ff_out.T], axis=1), jnp.concatenate([bias_rows] * 2, axis=1)]
    )
    ff_parts = around(after(ff_shard, x1, x2), tensor)
    ff_z = jnp.stack(ff_parts)
    ff_all = lax.all_gather(ff_z, "dp", axis=0)
    x_all = place_rows(x1, x2, swap(x1, dp), swap(x2, dp), k, z)
    x = lax.dynamic_slice_in_dim(x_all, k * rows, rows)
    g1, g2 = send_items(cotangent[:, 0], routes, z, ff_z)
    m1, m2 = send_items(memory[:, 0], routes, z, ff_z)
    mem = in_order(m1, m2, z)
    mem_all = both_cores(mem, swap(mem, dp), k)

    paths = jnp.concatenate([lengths[:, 0], parent[:, 0]], axis=1)
    other_paths = swap(paths, dp)
    my_path = pick(jnp.where(z % 2 == k, paths, other_paths), 0, z // 2)
    segs = lengths.shape[2]
    qaux, kaux = tree_aux(my_path[:segs], my_path[segs:], 2 * rows)

    q, key, val = (mm(x_all, w) for w in own_w)
    attn, lse = attn_fwd(q, key, val, qaux, kaux, True, 1024, 1024, deps=(ff_z,))
    mine = lax.dynamic_slice_in_dim(attn, k * rows, rows)
    other = swap(lax.dynamic_slice_in_dim(attn, (1 - k) * rows, rows), dp)
    attn_rows = both_cores(mine, other, k, 1)

    h1 = x + mm(attn_rows, out_t, NT)
    q2 = mm(h1, cq)
    k2, v2 = mm(mem_all, ck), mm(mem_all, cv)
    ctx, lse2 = attn_fwd(q2, k2, v2, qaux, kaux, False, 1024, 256)
    h2 = h1 + mm(ctx, cross_out_t, NT)
    g = in_order(g1, g2, z)
    output, dh2, ff_grads = ffn(h2, g, ff_all, ff_bias_out, z, drows)
    ff_mine = lax.psum_scatter(ff_grads, "dp", scatter_dimension=0, tiled=False)
    ff_blocks = ff_mine.reshape(drows + 8, tensor, 2 * fw).transpose(1, 0, 2)
    dctx = mm(dh2, cross_out_t)
    grad_cross_out_t = mm(dh2, ctx, TN)
    heads = width // HEAD
    pick_heads = (jnp.arange(width)[None, :] // HEAD == jnp.arange(heads)[:, None]).astype(F32)

    def deltas(a, b):
        prod = a * b
        n = prod.shape[1] // HEAD
        return lax.dot_general(
            pick_heads[:n, :prod.shape[1]], prod, NT, precision=lax.Precision.HIGHEST
        ).reshape(n // 2, 2, prod.shape[0])

    dq2, dk2, dv2 = attn_bwd(q2, k2, v2, dctx, lse2, deltas(dctx, ctx), qaux, kaux, False, 1024, 256)
    grad_cross_q = mm(h1, dq2, TN)
    grad_ck, grad_cv = mm(mem_all, dk2, TN), mm(mem_all, dv2, TN)
    mem_part = mm(dk2, ck, NT) + mm(dv2, cv, NT)
    mem_rows = mem_part.shape[0] // 2
    grad_mem = lax.dynamic_slice_in_dim(mem_part, k * mem_rows, mem_rows) + swap(
        lax.dynamic_slice_in_dim(mem_part, (1 - k) * mem_rows, mem_rows), dp
    )
    dh1 = dh2 + mm(dq2, cq, NT)
    dattn_rows = mm(dh1, out_t)
    grad_self_out_t = mm(dh1, attn_rows, TN)
    mine = lax.dynamic_slice_in_dim(dattn_rows, k * heads_wide, heads_wide, 1)
    other = swap(lax.dynamic_slice_in_dim(dattn_rows, (1 - k) * heads_wide, heads_wide, 1), dp)
    dattn = both_cores(mine, other, k)
    mid_blocks = reduce_over_dp(
        [grad_cross_q, grad_ck, grad_cv, grad_cross_out_t, grad_self_out_t], dp, tensor, ff_mine
    )
    out_back = return_items(output, routes, z)
    mem_back = return_items(grad_mem, routes, z)
    delta = deltas(dattn, attn)
    back = []
    for p in range(heads_wide // 128):
        deps = [] if p == 0 else list(out_back) + list(mem_back) + [back[0][0], ff_mine]
        back.append(attn_bwd(q, key, val, dattn, lse, delta, qaux, kaux, True, 1024, 512, pair=p, deps=deps))
    dq, dk, dv = (jnp.concatenate([b[i] for b in back], axis=1) for i in range(3))
    part = mm(dq, own_w[0], NT) + mm(dk, own_w[1], NT) + mm(dv, own_w[2], NT)
    dx = (
        dh1
        + lax.dynamic_slice_in_dim(part, k * rows, rows)
        + swap(lax.dynamic_slice_in_dim(part, (1 - k) * rows, rows), dp)
    )
    dq, dk, dv = (after(t, dx) for t in (dq, dk, dv))
    grad_qkv = [mm(x_all, t, TN) for t in (dq, dk, dv)]

    ff_sum = lax.psum_scatter(ff_blocks, "tensor", scatter_dimension=0, tiled=False)
    ff_sum = ff_sum.reshape(drows + 8, 2, 2, fw // 2)
    grad_ff_in = ff_sum[:drows, :, 0].reshape(drows, fw)
    grad_ff_out = ff_sum[:drows, :, 1].reshape(drows, fw)
    grad_bias_in, grad_bias_out = ff_sum[drows, :, 0].reshape(fw), ff_sum[drows + 1, :, 0].reshape(fw)
    mid_sums = reduce_over_tensor(mid_blocks, [hw] * 5)
    mid_a, mid_b = mid_sums[:3], mid_sums[3:]
    x_back = return_items(dx, routes, z)
    att = reduce_head_grads(grad_qkv, dp, tensor, d, z)
    return (
        both_batches(*out_back, z)[:, None],
        both_batches(*x_back, z)[:, None],
        both_batches(*mem_back, z)[:, None],
        jnp.stack(att),
        mid_b[1].T,
        mid_a[0],
        jnp.stack(mid_a[1:]),
        mid_b[0].T,
        grad_ff_in,
        grad_bias_in,
        grad_ff_out.T,
        grad_bias_out,
    )


def solution(mesh):
    rows4 = P(None, "dp", "tensor", None)
    col3, row2, col2 = P(None, "dp", "tensor"), P("tensor", "dp"), P("dp", "tensor")
    idx = P(None, "dp", None)
    return jax.shard_map(
        on_device,
        mesh=mesh,
        in_specs=(rows4, rows4, idx, idx, col3, row2, col2, col3, row2, col2, P("tensor"), row2, P(), rows4),
        out_specs=(rows4, rows4, rows4, col3, row2, col2, col3, row2, col2, P("tensor"), row2, P()),
        check_vma=False,
    )
```

```python
import functools

import jax
import jax.numpy as jnp
from jax import lax
from jax.experimental import pallas as pl
from jax.experimental.pallas import tpu as pltpu
from jax.sharding import PartitionSpec as P

HEAD = 64
LOG2E = 1.4426950408889634
LN2 = 0.6931471805599453
BF = jnp.bfloat16
F32 = jnp.float32
NT = (((1,), (1,)), ((), ()))
NN = (((1,), (0,)), ((), ()))


def dot(a, b, dims=NN):
    return lax.dot_general(a, b, dims, preferred_element_type=F32)


def split(x):
    hi = x.astype(BF).astype(F32)
    return hi, x - hi


def attn_fwd_kernel(q_ref, k_ref, v_ref, qa_ref, ka_ref, *refs, causal, qb, kb, rq, rk):
    o_ref, l_ref, qs, ks, vt = refs[-5:]
    lane = lax.broadcasted_iota(jnp.int32, (256, 128), 1)
    left = lane < HEAD

    def sel(a, b):
        return jnp.where(left, a, b)

    def build_q(i, _):
        r = pl.ds(pl.multiple_of(i * 256, 256), 256)
        x = q_ref[r, :] * (HEAD ** -0.5 * LOG2E)
        hi, lo = split(x)
        hir, lor = pltpu.roll(hi, HEAD, 1), pltpu.roll(lo, HEAD, 1)
        aux = qa_ref[r, :].astype(F32) if causal else jnp.zeros((256, 128), F32)
        qs[0, r, 0:128] = sel(hi, hir).astype(BF)
        qs[0, r, 128:256] = sel(lo, aux).astype(BF)
        qs[1, r, 0:128] = sel(hir, hi).astype(BF)
        qs[1, r, 128:256] = sel(lor, aux).astype(BF)
        return 0

    def build_k(i, _):
        r = pl.ds(pl.multiple_of(i * 256, 256), 256)
        hi, lo = split(k_ref[r, :])
        hir, lor = pltpu.roll(hi, HEAD, 1), pltpu.roll(lo, HEAD, 1)
        aux = ka_ref[r, :].astype(F32) if causal else jnp.zeros((256, 128), F32)
        ks[0, r, 0:128] = sel(hi, lor).astype(BF)
        ks[0, r, 128:256] = sel(hi, aux).astype(BF)
        ks[1, r, 0:128] = sel(hir, lo).astype(BF)
        ks[1, r, 128:256] = sel(hir, aux).astype(BF)
        hi, lo = split(v_ref[r, :])
        hir, lor = pltpu.roll(hi, HEAD, 1), pltpu.roll(lo, HEAD, 1)
        vt[0, :, r] = sel(hi, lor).T.astype(BF)
        vt[1, :, r] = sel(hir, lo).T.astype(BF)
        return 0

    lax.fori_loop(0, rq // 256, build_q, 0)
    lax.fori_loop(0, rk // 256, build_k, 0)

    def one_q(i, _):
        rows = pl.ds(pl.multiple_of(i * qb, qb), qb)

        def update(state, qh, h, keys, mask):
            m, s, acc = state
            st = dot(ks[h, keys, :], qh, NT)
            if mask is not None:
                kk = lax.broadcasted_iota(jnp.int32, st.shape, 0)
                qq = lax.broadcasted_iota(jnp.int32, st.shape, 1)
                st = jnp.where(kk - qq <= mask, st, -1e30)
            mn = jnp.maximum(m, jnp.max(st, axis=0, keepdims=True))
            p = jnp.exp2(st - mn)
            al = jnp.exp2(m - mn)
            s = s * al + jnp.sum(p, axis=0, keepdims=True)
            ph = p.astype(BF)
            plo = (p - ph.astype(F32)).astype(BF)
            return mn, s, acc * al + dot(vt[h, :, keys], ph) + dot(vt[h, :, keys], plo)

        qh = [qs[h, rows, :] for h in range(2)]

        def step(j, carry):
            keys = pl.ds(pl.multiple_of(j * kb, kb), kb)
            return tuple(update(carry[h], qh[h], h, keys, None) for h in range(2))

        init = (jnp.full((1, qb), -1e30, F32), jnp.zeros((1, qb), F32), jnp.zeros((128, qb), F32))
        carry = (init, init)
        if causal:
            carry = lax.fori_loop(0, i * qb // kb, step, carry)
            sub = qb // 2
            for j in range(2):
                keys = pl.ds(pl.multiple_of(i * qb + j * sub, sub), sub)
                new = []
                for h in range(2):
                    part = tuple(t[:, j * sub:] for t in carry[h])
                    part = update(part, qh[h][j * sub:], h, keys, 0)
                    if j:
                        part = tuple(jnp.concatenate([t[:, :sub], u], axis=1) for t, u in zip(carry[h], part))
                    new.append(part)
                carry = tuple(new)
        else:
            for j in range(rk // kb):
                carry = step(j, carry)
        outs = []
        for h in range(2):
            m, s, acc = carry[h]
            outs.append((acc[0:HEAD] + acc[HEAD:]) / s)
            l_ref[0, h:h + 1, rows] = m + jnp.log2(s)
        o_ref[rows, :] = jnp.concatenate(outs, axis=0).T
        return 0

    lax.fori_loop(0, rq // qb, one_q, 0)


def attn_fwd(q, k, v, qaux, kaux, causal, qb=512, kb=512, deps=()):
    rq, w = q.shape
    rk = k.shape[0]
    pairs = w // 128
    ra = qaux.shape[0]
    qspec = pl.BlockSpec((rq, 128), lambda p: (0, p))
    kspec = pl.BlockSpec((rk, 128), lambda p: (0, p))
    return pl.pallas_call(
        functools.partial(attn_fwd_kernel, causal=causal, qb=qb, kb=kb, rq=rq, rk=rk),
        grid=(pairs,),
        in_specs=[qspec, kspec, kspec,
                  pl.BlockSpec((ra, 128), lambda p: (0, 0)), pl.BlockSpec((ra, 128), lambda p: (0, 0))]
        + [pl.BlockSpec(memory_space=pl.ANY)] * len(deps),
        out_specs=[qspec, pl.BlockSpec((1, 2, rq), lambda p: (p, 0, 0))],
        out_shape=[jax.ShapeDtypeStruct((rq, w), F32), jax.ShapeDtypeStruct((pairs, 2, rq), F32)],
        scratch_shapes=[pltpu.VMEM((2, rq, 256), BF), pltpu.VMEM((2, rk, 256), BF), pltpu.VMEM((2, 128, rk), BF)],
        compiler_params=pltpu.CompilerParams(vmem_limit_bytes=28 << 20),
        cost_estimate=pl.CostEstimate(flops=(int(2e10) if causal else int(4e9)) * pairs, bytes_accessed=rq * w * 16, transcendentals=0),
        name="attn_fwd",
    )(q, k, v, qaux, kaux, *deps)


def attn_bwd_kernel(q_ref, k_ref, v_ref, do_ref, l_ref, d_ref, qa_ref, ka_ref, *refs, causal, qb, kb, rq, rk):
    dq_ref, dk_ref, dv_ref, qs, ks, kt, vs, dos, dka, dva = refs[-10:]
    lane = lax.broadcasted_iota(jnp.int32, (256, 128), 1)
    left = lane < HEAD

    def sel(a, b):
        return jnp.where(left, a, b)

    def build_q(i, _):
        r = pl.ds(pl.multiple_of(i * 256, 256), 256)
        hi, lo = split(q_ref[r, :] * (HEAD ** -0.5 * LOG2E))
        hir, lor = pltpu.roll(hi, HEAD, 1), pltpu.roll(lo, HEAD, 1)
        aux = qa_ref[r, :].astype(F32) if causal else jnp.zeros((256, 128), F32)
        qs[0, r, 0:128] = sel(hi, lor).astype(BF)
        qs[0, r, 128:256] = sel(hi, aux).astype(BF)
        qs[1, r, 0:128] = sel(hir, lo).astype(BF)
        qs[1, r, 128:256] = sel(hir, aux).astype(BF)
        hi, lo = split(do_ref[r, :])
        hir, lor = pltpu.roll(hi, HEAD, 1), pltpu.roll(lo, HEAD, 1)
        zero = jnp.zeros((256, 128), F32)
        dos[0, r, 0:128] = sel(hi, lor).astype(BF)
        dos[0, r, 128:256] = sel(hi, zero).astype(BF)
        dos[1, r, 0:128] = sel(hir, lo).astype(BF)
        dos[1, r, 128:256] = sel(hir, zero).astype(BF)
        return 0

    def build_k(i, _):
        r = pl.ds(pl.multiple_of(i * 256, 256), 256)
        hi, lo = split(k_ref[r, :])
        hir, lor = pltpu.roll(hi, HEAD, 1), pltpu.roll(lo, HEAD, 1)
        aux = ka_ref[r, :].astype(F32) if causal else jnp.zeros((256, 128), F32)
        ks[0, r, 0:128] = sel(hi, hir).astype(BF)
        ks[0, r, 128:256] = sel(lo, aux).astype(BF)
        ks[1, r, 0:128] = sel(hir, hi).astype(BF)
        ks[1, r, 128:256] = sel(lor, aux).astype(BF)
        kt[0, :, r] = sel(hi, lor).T.astype(BF)
        kt[1, :, r] = sel(hir, lo).T.astype(BF)
        hi, lo = split(v_ref[r, :])
        hir, lor = pltpu.roll(hi, HEAD, 1), pltpu.roll(lo, HEAD, 1)
        zero = jnp.zeros((256, 128), F32)
        vs[0, r, 0:128] = sel(hi, hir).astype(BF)
        vs[0, r, 128:256] = sel(lo, zero).astype(BF)
        vs[1, r, 0:128] = sel(hir, hi).astype(BF)
        vs[1, r, 128:256] = sel(lor, zero).astype(BF)
        dka[0, r, :] = zero
        dka[1, r, :] = zero
        dva[0, r, :] = zero
        dva[1, r, :] = zero
        return 0

    lax.fori_loop(0, rq // 256, build_q, 0)
    lax.fori_loop(0, rk // 256, build_k, 0)

    def one_q(i, _):
        rows = pl.ds(pl.multiple_of(i * qb, qb), qb)

        def update(acc, h, keys, cols, mask):
            qh = qs[h, cols, :]
            dh = dos[h, cols, :]
            st = dot(ks[h, keys, :], qh, NT)
            if mask is not None:
                kk = lax.broadcasted_iota(jnp.int32, st.shape, 0)
                qq = lax.broadcasted_iota(jnp.int32, st.shape, 1)
                st = jnp.where(kk - qq <= mask, st, -1e30)
            p = jnp.exp2(st - l_ref[0, h:h + 1, cols])
            ph = p.astype(BF)
            plo = (p - ph.astype(F32)).astype(BF)
            dhl = dh[:, 0:128]
            dva[h, keys, :] += dot(ph, dhl) + dot(plo, dhl)
            dp = dot(vs[h, keys, :], dh, NT)
            ds = p * (dp - d_ref[0, h:h + 1, cols])
            dsh = ds.astype(BF)
            dsl = (ds - dsh.astype(F32)).astype(BF)
            qhl = qh[:, 0:128]
            dka[h, keys, :] += dot(dsh, qhl) + dot(dsl, qhl)
            kth = kt[h, :, keys]
            return acc + dot(kth, dsh) + dot(kth, dsl)

        def step(j, carry):
            keys = pl.ds(pl.multiple_of(j * kb, kb), kb)
            return tuple(update(carry[h], h, keys, rows, None) for h in range(2))

        init = jnp.zeros((128, qb), F32)
        carry = (init, init)
        if causal:
            carry = lax.fori_loop(0, i * qb // kb, step, carry)
            sub = qb // 2
            for j in range(2):
                keys = pl.ds(pl.multiple_of(i * qb + j * sub, sub), sub)
                cols = pl.ds(pl.multiple_of(i * qb + j * sub, sub), qb - j * sub)
                new = []
                for h in range(2):
                    part = update(carry[h][:, j * sub:], h, keys, cols, 0)
                    if j:
                        part = jnp.concatenate([carry[h][:, :sub], part], axis=1)
                    new.append(part)
                carry = tuple(new)
        else:
            for j in range(rk // kb):
                carry = step(j, carry)
        outs = [(a[0:HEAD] + a[HEAD:]) * (HEAD ** -0.5) for a in carry]
        dq_ref[rows, :] = jnp.concatenate(outs, axis=0).T
        return 0

    lax.fori_loop(0, rq // qb, one_q, 0)

    def finish(i, _):
        r = pl.ds(pl.multiple_of(i * 256, 256), 256)
        a, b = dka[0, r, :], dka[1, r, :]
        dk_ref[r, :] = sel(a + pltpu.roll(a, HEAD, 1), b + pltpu.roll(b, HEAD, 1)) * LN2
        a, b = dva[0, r, :], dva[1, r, :]
        dv_ref[r, :] = sel(a + pltpu.roll(a, HEAD, 1), b + pltpu.roll(b, HEAD, 1))
        return 0

    lax.fori_loop(0, rk // 256, finish, 0)


def attn_bwd(q, k, v, do, lse, delta, qaux, kaux, causal, qb=512, kb=512, pair=None, deps=(), prev=()):
    rq, w = q.shape
    rk = k.shape[0]
    pairs = 1 if pair is not None else w // 128
    first = pair or 0
    deps = list(prev) + list(deps)
    ra = qaux.shape[0]
    qspec = pl.BlockSpec((rq, 128), lambda p: (0, p + first))
    kspec = pl.BlockSpec((rk, 128), lambda p: (0, p + first))
    lspec = pl.BlockSpec((1, 2, rq), lambda p: (p + first, 0, 0))
    aspec = pl.BlockSpec((ra, 128), lambda p: (0, 0))
    return pl.pallas_call(
        functools.partial(attn_bwd_kernel, causal=causal, qb=qb, kb=kb, rq=rq, rk=rk),
        grid=(pairs,),
        in_specs=[qspec, kspec, kspec, qspec, lspec, lspec, aspec, aspec]
        + [pl.BlockSpec(memory_space=pl.ANY)] * len(deps),
        out_specs=[qspec, kspec, kspec],
        out_shape=[jax.ShapeDtypeStruct((n, w), F32) for n in (rq, rk, rk)],
        input_output_aliases={8 + i: i for i in range(len(prev))},
        scratch_shapes=[pltpu.VMEM((2, rq, 256), BF), pltpu.VMEM((2, rk, 256), BF), pltpu.VMEM((2, 128, rk), BF),
                        pltpu.VMEM((2, rk, 256), BF), pltpu.VMEM((2, rq, 256), BF),
                        pltpu.VMEM((2, rk, 128), F32), pltpu.VMEM((2, rk, 128), F32)],
        compiler_params=pltpu.CompilerParams(vmem_limit_bytes=40 << 20),
        cost_estimate=pl.CostEstimate(flops=(int(3.4e10) if causal else int(5e9)) * pairs, bytes_accessed=rq * w * 32, transcendentals=0),
        name="attn_bwd",
    )(q, k, v, do, lse, delta, qaux, kaux, *deps)


def attn_bwd_inputs_kernel(q_ref, k_ref, v_ref, do_ref, l_ref, d_ref, qa_ref, ka_ref, x_ref, wq_ref, wk_ref, wv_ref,
                           *refs, qb, kb, rq, rk, more):
    part_ref, g_ref, dq, dk, dv = refs[-12:-7]
    scratch = refs[-7:]
    attn_bwd_kernel(
        q_ref, k_ref, v_ref, do_ref, l_ref, d_ref, qa_ref, ka_ref, dq, dk, dv, *scratch,
        causal=True, qb=qb, kb=kb, rq=rq, rk=rk,
    )
    weights = parts2(jnp.concatenate([wq_ref[...], wk_ref[...], wv_ref[...]], axis=1))
    step = 512
    g_ref[...] = jnp.zeros(g_ref.shape, F32)

    def body(i, _):
        r = pl.ds(pl.multiple_of(i * step, step), step)
        grads = parts2(jnp.concatenate([dq[r, :], dk[r, :], dv[r, :]], axis=1))
        new = dot3(grads, weights, NT)
        part_ref[r, :] = new + refs[0][r, :] if more else new
        g_ref[...] += dot3(parts2(x_ref[r, :].T), grads)
        return 0

    lax.fori_loop(0, rq // step, body, 0)


def attn_bwd_inputs(q, k, v, do, lse, delta, qaux, kaux, x, weights, qb, kb, pair, prev=None, deps=()):
    rows, w = q.shape
    width = x.shape[1]
    one = pl.Buffered(1)
    qspec = pl.BlockSpec((rows, 128), lambda p: (0, pair), pipeline_mode=one)
    lspec = pl.BlockSpec((1, 2, rows), lambda p: (pair, 0, 0))
    aspec = pl.BlockSpec((rows, 128), lambda p: (0, 0), pipeline_mode=one)
    wspec = pl.BlockSpec((width, 128), lambda p: (0, pair), pipeline_mode=one)
    xspec = pl.BlockSpec((rows, width), lambda p: (0, 0), pipeline_mode=one)
    first = () if prev is None else (prev,)
    return pl.pallas_call(
        functools.partial(attn_bwd_inputs_kernel, qb=qb, kb=kb, rq=rows, rk=rows, more=bool(first)),
        grid=(1,),
        in_specs=[qspec] * 4 + [lspec, lspec, aspec, aspec, xspec, wspec, wspec, wspec] + [xspec] * len(first)
        + [pl.BlockSpec(memory_space=pl.ANY)] * len(deps),
        out_specs=[xspec, pl.BlockSpec((width, 384), lambda p: (0, 0), pipeline_mode=one)],
        out_shape=[jax.ShapeDtypeStruct((rows, width), F32), jax.ShapeDtypeStruct((width, 384), F32)],
        scratch_shapes=[pltpu.VMEM((rows, 128), F32)] * 3
        + [pltpu.VMEM((2, rows, 256), BF), pltpu.VMEM((2, rows, 256), BF), pltpu.VMEM((2, 128, rows), BF),
           pltpu.VMEM((2, rows, 256), BF), pltpu.VMEM((2, rows, 256), BF),
           pltpu.VMEM((2, rows, 128), F32), pltpu.VMEM((2, rows, 128), F32)],
        compiler_params=pltpu.CompilerParams(vmem_limit_bytes=48 << 20),
        cost_estimate=pl.CostEstimate(flops=int(4e10), bytes_accessed=rows * w * 32, transcendentals=0),
        name="attn_bwd_inputs",
    )(q, k, v, do, lse, delta, qaux, kaux, x, *weights, *first, *deps)


def tree_aux(lengths, parent, n):
    segs = lengths.shape[0]
    ends = jnp.cumsum(lengths)
    places = jnp.arange(n, dtype=jnp.int32)
    seg = jnp.sum((places[:, None] >= ends[None, :-1]).astype(jnp.int32), axis=1)
    labels = jnp.arange(segs, dtype=jnp.int32)
    onehot = seg[:, None] == labels[None, :]
    up1 = jnp.sum(jnp.where(onehot, parent[None, :], 0), axis=1)
    up2 = jnp.sum(jnp.where(up1[:, None] == labels[None, :], parent[None, :], 0), axis=1)
    lab = jnp.arange(128, dtype=jnp.int32)[None, :] - HEAD
    inside = (lab >= 0) & (lab < segs)
    sg = seg[:, None]
    kaux = jnp.where(inside & (lab == sg), 1.0, 0.0).astype(BF)
    ok = (lab == sg) | ((sg > 0) & ((lab == up1[:, None]) | (lab == up2[:, None])))
    qaux = jnp.where(inside & ~ok, -1e30, 0.0).astype(BF)
    return qaux, kaux


HIGH = lax.Precision.HIGH
TN = (((0,), (0,)), ((), ()))
BOTH = ("dp", "tensor")
ANY = pl.BlockSpec(memory_space=pl.ANY)
VMEM = pl.BlockSpec(memory_space=pltpu.VMEM)
SMEM = pl.BlockSpec(memory_space=pltpu.SMEM)


def mm(a, b, dims=NN):
    return lax.dot_general(a, b, dims, precision=HIGH, preferred_element_type=F32)


def nothing(*refs):
    pass


def corner(x):
    return x if x.ndim < 2 else x.reshape((-1,) + x.shape[-1:])[:8, :128]


def after(x, *others):
    return pl.pallas_call(
        nothing,
        in_specs=[ANY] * (1 + len(others)),
        out_specs=ANY,
        out_shape=jax.ShapeDtypeStruct(x.shape, x.dtype),
        input_output_aliases={0: 0},
        name="after",
    )(x, *others)


def flip_bit(size, bit):
    return [(i, i ^ (1 << bit)) for i in range(size)]


def turn(size, by):
    return [(i, (i + by) % size) for i in range(size)]


def pick(x, axis, index):
    return lax.dynamic_index_in_dim(x, index, axis, keepdims=False)


def item_routes(dp, tensor):
    routes = []
    for step in range(2):
        pairs = []
        for c in range(dp // 2):
            for t in range(2):
                for z in range(tensor):
                    b = (z + step) % 2
                    pairs.append(((2 * c + t) * tensor + z, (2 * c + z // 2) * tensor + 2 * b + t))
        routes.append(pairs)
    return routes


def send_items(x, routes, z, *others):
    first, second = pick(x, 0, z % 2), pick(x, 0, 1 - z % 2)
    if others:
        first, second = after(first, *others), after(second, *others)
    return lax.ppermute(first, BOTH, routes[0]), lax.ppermute(second, BOTH, routes[1])


def in_order(first, second, z):
    return jnp.where(z // 2 == 0, jnp.concatenate([first, second]), jnp.concatenate([second, first]))


def return_items(rows, routes, z, between=None):
    half = rows.shape[0] // 2
    b = z // 2
    back = [[(t, s) for s, t in r] for r in routes]
    first = lax.ppermute(lax.dynamic_slice_in_dim(rows, b * half, half), BOTH, back[0])
    second = lax.dynamic_slice_in_dim(rows, (1 - b) * half, half)
    if between is not None:
        second = after(second, first, between)
    return first, lax.ppermute(second, BOTH, back[1])


def both_batches(first, second, z):
    return jnp.where(z % 2 == 0, jnp.stack([first, second]), jnp.stack([second, first]))


def swap(x, dp):
    return lax.ppermute(x, "dp", flip_bit(dp, 0))


def both_cores(mine, other, k, axis=0):
    return jnp.where(
        k == 0, jnp.concatenate([mine, other], axis), jnp.concatenate([other, mine], axis)
    )


def rows_kernel(who_ref, a_ref, b_ref, c_ref, d_ref, o_ref):
    k, m = who_ref[0], who_ref[1]
    half = a_ref.shape[0]
    for ref, core, which in ((a_ref, k, m), (b_ref, k, 1 - m), (c_ref, 1 - k, m), (d_ref, 1 - k, 1 - m)):
        o_ref[pl.ds(pl.multiple_of((2 * core + which) * half, half), half), :] = ref[...]


def place_rows(first, second, other_first, other_second, k, z):
    half, width = first.shape
    who = jnp.stack([k, z // 2]).astype(jnp.int32)
    return pl.pallas_call(
        rows_kernel,
        in_specs=[SMEM, VMEM, VMEM, VMEM, VMEM],
        out_specs=VMEM,
        out_shape=jax.ShapeDtypeStruct((4 * half, width), F32),
        compiler_params=pltpu.CompilerParams(vmem_limit_bytes=32 << 20),
        cost_estimate=pl.CostEstimate(flops=0, bytes_accessed=32 * half * width, transcendentals=0),
        name="place_rows",
    )(who, first, second, other_first, other_second)


ROOT_HALF = 0.7071067811865476
NORMAL_PEAK = 0.3989422804014327


def parts2(x):
    hi = x.astype(BF)
    return hi, (x - hi.astype(F32)).astype(BF)


def dot3(a, b, dims=NN):
    return dot(a[0], b[0], dims) + (dot(a[0], b[1], dims) + dot(a[1], b[0], dims))


def ffn_kernel(z_ref, h_ref, g_ref, wi_ref, wo_ref, bo_ref, out_ref, dh_ref, gr_ref, bi_ref, go_ref,
               hh, hl, gh, gl, hth, htl, gth, gtl, ah, al, dh, dl, *, rb, drows):
    j = pl.program_id(0)
    n = h_ref.shape[0]

    @pl.when(j == 0)
    def _():
        for r in range(n // rb):
            rows = slice(r * rb, (r + 1) * rb)
            for ref, h, l, th, tl in ((h_ref, hh, hl, hth, htl), (g_ref, gh, gl, gth, gtl)):
                x = ref[rows, :]
                h[rows, :], l[rows, :] = parts2(x)
                th[:, rows], tl[:, rows] = parts2(x.T)
            out_ref[rows, :] = h_ref[rows, :] + bo_ref[0:1, :]
            dh_ref[rows, :] = g_ref[rows, :]

    dp = wi_ref.shape[0]
    wide = wi_ref.shape[3]
    wi = parts2(wi_ref[:, 0, 0:drows, :].reshape(dp * drows, wide))
    wo = parts2(wo_ref[:, 0, 0:drows, :].reshape(dp * drows, wide))
    bias = wi_ref[0, 0, drows:drows + 1, :]
    total = jnp.zeros((1, wide), F32)
    for r in range(n // rb):
        rows = slice(r * rb, (r + 1) * rb)
        u = dot3((hh[rows, :], hl[rows, :]), wi) + bias
        gz = dot3((gh[rows, :], gl[rows, :]), wo)
        cdf = 0.5 * (1.0 + lax.erf(u * ROOT_HALF))
        act = u * cdf
        du = gz * (cdf + u * (NORMAL_PEAK * jnp.exp(-0.5 * u * u)))
        total = total + jnp.sum(du, axis=0, keepdims=True)
        act, du = parts2(act), parts2(du)
        ah[rows, :], al[rows, :] = act
        dh[rows, :], dl[rows, :] = du
        out_ref[rows, :] += dot3(act, wo, NT)
        dh_ref[rows, :] += dot3(du, wi, NT)
    gr_ref[:, :, 0:wide] = dot3((hth[...], htl[...]), (dh[...], dl[...])).reshape(dp, drows, wide)
    gr_ref[:, :, wide:] = dot3((gth[...], gtl[...]), (ah[...], al[...])).reshape(dp, drows, wide)
    bi_ref[0:1, :] = total

    @pl.when(j == 0)
    def _():
        go_ref[0:1, :] = jnp.sum(g_ref[...], axis=0, keepdims=True)


def ffn(h2, g, ff_all, bias_out, z, drows):
    n, width = h2.shape
    dp, tensor, high, both = ff_all.shape
    wide = both // 4
    steps = 2 * tensor
    full = lambda: pl.BlockSpec((n, width), lambda j, z: (0, 0))
    return pl.pallas_call(
        functools.partial(ffn_kernel, rb=512, drows=drows),
        grid_spec=pltpu.PrefetchScalarGridSpec(
            num_scalar_prefetch=1,
            grid=(steps,),
            in_specs=[
                full(), full(),
                pl.BlockSpec((dp, 1, high, wide), lambda j, z: (0, (z[0] + tensor - j // 2) % tensor, 0, j % 2)),
                pl.BlockSpec((dp, 1, high, wide), lambda j, z: (0, (z[0] + tensor - j // 2) % tensor, 0, 2 + j % 2)),
                pl.BlockSpec((1, width), lambda j, z: (0, 0)),
            ],
            out_specs=[
                full(), full(), pl.BlockSpec((dp, drows, 2 * wide), lambda j, z: (0, 0, j)),
                pl.BlockSpec((1, wide), lambda j, z: (0, j)), pl.BlockSpec((1, width), lambda j, z: (0, 0)),
            ],
            scratch_shapes=[pltpu.VMEM((n, width), BF)] * 4 + [pltpu.VMEM((width, n), BF)] * 4
            + [pltpu.VMEM((n, wide), BF)] * 4,
        ),
        out_shape=[
            jax.ShapeDtypeStruct((n, width), F32),
            jax.ShapeDtypeStruct((n, width), F32),
            jax.ShapeDtypeStruct((dp, drows, 2 * wide * steps), F32),
            jax.ShapeDtypeStruct((1, wide * steps), F32),
            jax.ShapeDtypeStruct((1, width), F32),
        ],
        compiler_params=pltpu.CompilerParams(vmem_limit_bytes=48 << 20),
        cost_estimate=pl.CostEstimate(flops=int(5e10), bytes_accessed=30 << 20, transcendentals=0),
        name="ffn",
    )(z[None].astype(jnp.int32), h2, g, ff_all, ff_all, bias_out[None])


def around(x, tensor):
    return [x] + [lax.ppermute(x, "tensor", turn(tensor, s)) for s in range(1, tensor)]


def place_kernel(who_ref, g_ref, *outs, widths, own):
    k, z = who_ref[0], who_ref[1]
    tensor = g_ref.shape[1]
    half = tensor // 2
    for s in range(tensor):
        col = (z + tensor - s) % tensor
        start = 0
        for o, w, only in zip(outs, widths, own):
            def copy(c, o=o, w=w, s=s, start=start):
                o[:, pl.ds(pl.multiple_of(c * w, w), w)] = g_ref[0, s, :, start:start + w]

            if only:
                pl.when(col // half == k)(functools.partial(copy, col % half))
            else:
                copy(col)
            start += w


def place_weights(g, widths, own, k, z):
    dp, tensor, rows, wide = g.shape
    who = jnp.stack([k, z]).astype(jnp.int32)
    cols = [w * (tensor // 2 if o else tensor) for o, w in zip(own, widths)]
    return pl.pallas_call(
        functools.partial(place_kernel, widths=widths, own=own),
        grid=(dp,),
        in_specs=[SMEM, pl.BlockSpec((1, tensor, rows, wide), lambda i: (i, 0, 0, 0))],
        out_specs=[pl.BlockSpec((rows, c), lambda i: (i, 0)) for c in cols],
        out_shape=[jax.ShapeDtypeStruct((dp * rows, c), F32) for c in cols],
        cost_estimate=pl.CostEstimate(flops=0, bytes_accessed=8 * dp * tensor * rows * wide, transcendentals=0),
        name="place_weights",
    )(who, g)


def halve(cur, seq, dp, d):
    left = sorted(seq, reverse=True)
    cur = cur.reshape((2,) * len(left) + cur.shape[1:])
    for bit in seq:
        axis = left.index(bit)
        mine = (d >> bit) & 1
        sent = lax.ppermute(pick(cur, axis, 1 - mine), "dp", flip_bit(dp, bit))
        cur = pick(cur, axis, mine) + sent
        left.remove(bit)
    return cur


def along_z(parts, tensor, z, *others):
    total = parts(z)
    for s in range(1, tensor):
        part = parts((z + s) % tensor)
        if others:
            part = after(part, *others)
        total = total + lax.ppermute(part, "tensor", turn(tensor, s))
    return total


def column_block(x, i, tensor):
    w = x.shape[-1] // tensor
    return lax.dynamic_slice_in_dim(x, i * w, w, x.ndim - 1)


def reduce_over_dp(mats, extra, dp, *others):
    whole = jnp.concatenate([m.reshape(dp, m.shape[0] // dp, m.shape[1]) for m in mats], axis=2)
    whole = jnp.concatenate([whole, jnp.broadcast_to(extra[None], (dp,) + extra.shape)], axis=1)
    return lax.psum_scatter(after(whole, *others), "dp", scatter_dimension=0, tiled=False)


def reduce_head_grads(mats, dp, tensor, d, z):
    bits = dp.bit_length() - 1
    k = d % 2
    chains = []
    for u, m in enumerate(mats):
        seq = list(range(1, bits))
        if u % 2:
            seq = seq[::-1]
        m = m.reshape(dp // 2, 2, m.shape[0] // dp, m.shape[1])
        both = jnp.stack([pick(m, 1, k), swap(pick(m, 1, 1 - k), dp)], axis=1)
        chains.append(halve(both, seq, dp, d))
    return jnp.stack(chains)


def on_device(
    inputs, memory, lengths, parent, self_qkv, self_out, cross_q, cross_kv, cross_out,
    ff_in, ff_bias_in, ff_out, ff_bias_out, cotangent,
):
    dp, tensor = lax.axis_size("dp"), lax.axis_size("tensor")
    d, z = lax.axis_index("dp"), lax.axis_index("tensor")
    k = d % 2
    routes = item_routes(dp, tensor)
    rows = inputs.shape[2] * 2
    width = inputs.shape[3]
    heads_wide = width // 2
    hw = self_qkv.shape[2]
    fw = ff_in.shape[1]
    drows = ff_in.shape[0]

    shard = jnp.concatenate(
        [self_qkv[0], self_qkv[1], self_qkv[2], self_out.T, cross_q, cross_kv[0], cross_kv[1], cross_out.T], axis=1
    )
    x_first, x_second = pick(inputs[:, 0], 0, z % 2), pick(inputs[:, 0], 0, 1 - z % 2)
    g_first, g_second = pick(cotangent[:, 0], 0, z % 2), pick(cotangent[:, 0], 0, 1 - z % 2)
    paths = jnp.concatenate([lengths[:, 0], parent[:, 0]], axis=1)
    other_paths = swap(paths, dp)
    m1, m2 = send_items(memory[:, 0], routes, z)
    parts = around(after(shard, x_first, x_second), tensor)
    weights = lax.all_gather(after(jnp.stack(parts), m1, m2, other_paths), "dp", axis=0)
    x1 = lax.ppermute(after(x_first, *parts[1:]), BOTH, routes[0])
    x2 = lax.ppermute(after(x_second, *parts[1:]), BOTH, routes[1])
    mem = in_order(m1, m2, z)
    mem_all = both_cores(mem, swap(mem, dp), k)

    my_path = pick(jnp.where(z % 2 == k, paths, other_paths), 0, z // 2)
    segs = lengths.shape[2]
    qaux, kaux = tree_aux(my_path[:segs], my_path[segs:], 2 * rows)

    bias_rows = jnp.concatenate([ff_bias_in[None], jnp.zeros((7, fw), F32)])
    ff_shard = jnp.concatenate(
        [jnp.concatenate([ff_in, ff_out.T], axis=1), jnp.concatenate([bias_rows] * 2, axis=1)]
    )
    ff_parts = around(after(ff_shard, x1, x2, mem_all, qaux, kaux, corner(g_first), corner(g_second)), tensor)
    wq, wk, wv, out_t, cq, ck, cv, cross_out_t = place_weights(
        weights, [hw] * 8, [True] * 3 + [False] * 5, k, z
    )
    own_w = [wq, wk, wv]
    x_all = place_rows(x1, x2, swap(x1, dp), swap(x2, dp), k, z)
    x = lax.dynamic_slice_in_dim(x_all, k * rows, rows)
    q, key, val = (mm(x_all, w) for w in own_w)
    ff_z = jnp.stack([ff_parts[0]] + [after(t, corner(q), corner(key), corner(val)) for t in ff_parts[1:]])
    ff_all = lax.all_gather(ff_z, "dp", axis=0)
    g1 = lax.ppermute(after(g_first, ff_z), BOTH, routes[0])
    g2 = lax.ppermute(after(g_second, ff_z), BOTH, routes[1])

    attn, lse = attn_fwd(q, key, val, qaux, kaux, True, 1024, 1024, deps=(ff_z,))
    mine = lax.dynamic_slice_in_dim(attn, k * rows, rows)
    other = swap(lax.dynamic_slice_in_dim(attn, (1 - k) * rows, rows), dp)
    attn_rows = both_cores(mine, other, k, 1)

    h1 = x + mm(attn_rows, out_t, NT)
    q2 = mm(h1, cq)
    k2, v2 = mm(mem_all, ck), mm(mem_all, cv)
    ctx, lse2 = attn_fwd(q2, k2, v2, qaux, kaux, False, 1024, 256)
    h2 = h1 + mm(ctx, cross_out_t, NT)
    g = in_order(g1, g2, z)
    output, dh2, ff_grads, du_sum, g_sum = ffn(h2, g, ff_all, ff_bias_out, z, drows)
    ff_mine = lax.psum_scatter(ff_grads, "dp", scatter_dimension=0, tiled=False)
    cut = fw // hw
    spare = jnp.zeros((1, (5 - cut) * tensor * hw), F32)
    bias_rows = jnp.concatenate([
        jnp.concatenate([du_sum.reshape(tensor, cut, hw).transpose(1, 0, 2).reshape(1, -1), spare], axis=1),
        jnp.concatenate([jnp.repeat(g_sum.reshape(cut, 1, hw), tensor, axis=1).reshape(1, -1), spare], axis=1),
        jnp.zeros((6, 5 * tensor * hw), F32),
    ])
    dctx = mm(dh2, cross_out_t)
    grad_cross_out_t = mm(dh2, ctx, TN)
    heads = width // HEAD
    pick_heads = (jnp.arange(width)[None, :] // HEAD == jnp.arange(heads)[:, None]).astype(F32)

    def deltas(a, b):
        prod = a * b
        n = prod.shape[1] // HEAD
        return lax.dot_general(
            pick_heads[:n, :prod.shape[1]], prod, NT, precision=lax.Precision.HIGHEST
        ).reshape(n // 2, 2, prod.shape[0])

    dq2, dk2, dv2 = attn_bwd(q2, k2, v2, dctx, lse2, deltas(dctx, ctx), qaux, kaux, False, 1024, 256)
    grad_cross_q = mm(h1, dq2, TN)
    grad_ck, grad_cv = mm(mem_all, dk2, TN), mm(mem_all, dv2, TN)
    mem_part = mm(dk2, ck, NT) + mm(dv2, cv, NT)
    mem_rows = mem_part.shape[0] // 2
    grad_mem = lax.dynamic_slice_in_dim(mem_part, k * mem_rows, mem_rows) + swap(
        lax.dynamic_slice_in_dim(mem_part, (1 - k) * mem_rows, mem_rows), dp
    )
    dh1 = dh2 + mm(dq2, cq, NT)
    dattn_rows = mm(dh1, out_t)
    grad_self_out_t = mm(dh1, attn_rows, TN)
    mine = lax.dynamic_slice_in_dim(dattn_rows, k * heads_wide, heads_wide, 1)
    other = swap(lax.dynamic_slice_in_dim(dattn_rows, (1 - k) * heads_wide, heads_wide, 1), dp)
    dattn = both_cores(mine, other, k)
    mid_mine = reduce_over_dp(
        [grad_cross_q, grad_ck, grad_cv, grad_cross_out_t, grad_self_out_t], bias_rows, dp, ff_mine
    )
    ff_sum = along_z(lambda i: column_block(ff_mine, i, tensor), tensor, z)
    out_back = return_items(output, routes, z)
    delta = deltas(dattn, attn)
    part, head_grads = None, []
    for p in range(heads_wide // 128):
        deps = [ff_mine]
        if p:
            ff_sum, *out_back = (after(t, corner(part)) for t in [ff_sum, *out_back])
            deps = [corner(t) for t in [ff_sum, *out_back]]
        part, got = attn_bwd_inputs(
            q, key, val, dattn, lse, delta, qaux, kaux, x_all, own_w, 1024, 512, p, prev=part, deps=deps
        )
        head_grads.append(got)
    dx = (
        dh1
        + lax.dynamic_slice_in_dim(part, k * rows, rows)
        + swap(lax.dynamic_slice_in_dim(part, (1 - k) * rows, rows), dp)
    )
    def mid_parts(i):
        return jnp.concatenate(
            [column_block(mid_mine[:, n * width:(n + 1) * width], i, tensor) for n in range(5)], axis=1
        )

    mid_sum = along_z(mid_parts, tensor, z)
    x_back = return_items(dx, routes, z, between=corner(mid_sum))
    head_grads = [after(t, corner(mid_sum)) for t in head_grads]
    mem_back = return_items(after(grad_mem, corner(mid_sum)), routes, z)
    ff_sum = ff_sum.reshape(drows, 2, 2, fw // 2)
    grad_ff_in = ff_sum[:, :, 0].reshape(drows, fw)
    grad_ff_out = ff_sum[:, :, 1].reshape(drows, fw)

    mid = [mid_sum[:drows, n * hw:(n + 1) * hw] for n in range(5)]
    grad_bias_in, grad_bias_out = mid_sum[drows, :fw], mid_sum[drows + 1, :fw]
    head_sums = reduce_head_grads(head_grads, dp, tensor, d, z)
    half = tensor // 2
    att = along_z(
        lambda i: pick(pick(head_sums, 0, i % half), 0, (i // half + k) % 2), tensor, z,
    )
    att = [att[:, n * hw:(n + 1) * hw] for n in range(3)]
    return (
        both_batches(*out_back, z)[:, None],
        both_batches(*x_back, z)[:, None],
        both_batches(*mem_back, z)[:, None],
        jnp.stack(att),
        mid[4].T,
        mid[0],
        jnp.stack(mid[1:3]),
        mid[3].T,
        grad_ff_in,
        grad_bias_in,
        grad_ff_out.T,
        grad_bias_out,
    )


def solution(mesh):
    rows4 = P(None, "dp", "tensor", None)
    col3, row2, col2 = P(None, "dp", "tensor"), P("tensor", "dp"), P("dp", "tensor")
    idx = P(None, "dp", None)
    return jax.shard_map(
        on_device,
        mesh=mesh,
        in_specs=(rows4, rows4, idx, idx, col3, row2, col2, col3, row2, col2, P("tensor"), row2, P(), rows4),
        out_specs=(rows4, rows4, rows4, col3, row2, col2, col3, row2, col2, P("tensor"), row2, P()),
        check_vma=False,
    )
```

```python
import functools

import jax
import jax.numpy as jnp
from jax import lax
from jax.experimental import pallas as pl
from jax.experimental.pallas import tpu as pltpu
from jax.sharding import PartitionSpec as P

HEAD = 64
LOG2E = 1.4426950408889634
LN2 = 0.6931471805599453
BF = jnp.bfloat16
F32 = jnp.float32
NT = (((1,), (1,)), ((), ()))
NN = (((1,), (0,)), ((), ()))


def dot(a, b, dims=NN):
    return lax.dot_general(a, b, dims, preferred_element_type=F32)


def split(x):
    hi = x.astype(BF).astype(F32)
    return hi, x - hi


def attn_fwd_kernel(q_ref, k_ref, v_ref, qa_ref, ka_ref, *refs, causal, qb, kb, rq, rk):
    o_ref, l_ref, qs, ks, vt = refs[-5:]
    lane = lax.broadcasted_iota(jnp.int32, (256, 128), 1)
    left = lane < HEAD

    def sel(a, b):
        return jnp.where(left, a, b)

    def build_q(i, _):
        r = pl.ds(pl.multiple_of(i * 256, 256), 256)
        x = q_ref[r, :] * (HEAD ** -0.5 * LOG2E)
        hi, lo = split(x)
        hir, lor = pltpu.roll(hi, HEAD, 1), pltpu.roll(lo, HEAD, 1)
        aux = qa_ref[r, :].astype(F32) if causal else jnp.zeros((256, 128), F32)
        qs[0, r, 0:128] = sel(hi, hir).astype(BF)
        qs[0, r, 128:256] = sel(lo, aux).astype(BF)
        qs[1, r, 0:128] = sel(hir, hi).astype(BF)
        qs[1, r, 128:256] = sel(lor, aux).astype(BF)
        return 0

    def build_k(i, _):
        r = pl.ds(pl.multiple_of(i * 256, 256), 256)
        hi, lo = split(k_ref[r, :])
        hir, lor = pltpu.roll(hi, HEAD, 1), pltpu.roll(lo, HEAD, 1)
        aux = ka_ref[r, :].astype(F32) if causal else jnp.zeros((256, 128), F32)
        ks[0, r, 0:128] = sel(hi, lor).astype(BF)
        ks[0, r, 128:256] = sel(hi, aux).astype(BF)
        ks[1, r, 0:128] = sel(hir, lo).astype(BF)
        ks[1, r, 128:256] = sel(hir, aux).astype(BF)
        hi, lo = split(v_ref[r, :])
        hir, lor = pltpu.roll(hi, HEAD, 1), pltpu.roll(lo, HEAD, 1)
        vt[0, :, r] = sel(hi, lor).T.astype(BF)
        vt[1, :, r] = sel(hir, lo).T.astype(BF)
        return 0

    lax.fori_loop(0, rq // 256, build_q, 0)
    lax.fori_loop(0, rk // 256, build_k, 0)

    def one_q(i, _):
        rows = pl.ds(pl.multiple_of(i * qb, qb), qb)

        def update(state, qh, h, keys, mask):
            m, s, acc = state
            st = dot(ks[h, keys, :], qh, NT)
            if mask is not None:
                kk = lax.broadcasted_iota(jnp.int32, st.shape, 0)
                qq = lax.broadcasted_iota(jnp.int32, st.shape, 1)
                st = jnp.where(kk - qq <= mask, st, -1e30)
            mn = jnp.maximum(m, jnp.max(st, axis=0, keepdims=True))
            p = jnp.exp2(st - mn)
            al = jnp.exp2(m - mn)
            s = s * al + jnp.sum(p, axis=0, keepdims=True)
            ph = p.astype(BF)
            plo = (p - ph.astype(F32)).astype(BF)
            return mn, s, acc * al + dot(vt[h, :, keys], ph) + dot(vt[h, :, keys], plo)

        qh = [qs[h, rows, :] for h in range(2)]

        def step(j, carry):
            keys = pl.ds(pl.multiple_of(j * kb, kb), kb)
            return tuple(update(carry[h], qh[h], h, keys, None) for h in range(2))

        init = (jnp.full((1, qb), -1e30, F32), jnp.zeros((1, qb), F32), jnp.zeros((128, qb), F32))
        carry = (init, init)
        if causal:
            carry = lax.fori_loop(0, i * qb // kb, step, carry)
            sub = qb // 2
            for j in range(2):
                keys = pl.ds(pl.multiple_of(i * qb + j * sub, sub), sub)
                new = []
                for h in range(2):
                    part = tuple(t[:, j * sub:] for t in carry[h])
                    part = update(part, qh[h][j * sub:], h, keys, 0)
                    if j:
                        part = tuple(jnp.concatenate([t[:, :sub], u], axis=1) for t, u in zip(carry[h], part))
                    new.append(part)
                carry = tuple(new)
        else:
            for j in range(rk // kb):
                carry = step(j, carry)
        outs = []
        for h in range(2):
            m, s, acc = carry[h]
            outs.append((acc[0:HEAD] + acc[HEAD:]) / s)
            l_ref[0, h:h + 1, rows] = m + jnp.log2(s)
        o_ref[rows, :] = jnp.concatenate(outs, axis=0).T
        return 0

    lax.fori_loop(0, rq // qb, one_q, 0)


def attn_fwd(q, k, v, qaux, kaux, causal, qb=512, kb=512, deps=()):
    rq, w = q.shape
    rk = k.shape[0]
    pairs = w // 128
    ra = qaux.shape[0]
    qspec = pl.BlockSpec((rq, 128), lambda p: (0, p))
    kspec = pl.BlockSpec((rk, 128), lambda p: (0, p))
    return pl.pallas_call(
        functools.partial(attn_fwd_kernel, causal=causal, qb=qb, kb=kb, rq=rq, rk=rk),
        grid=(pairs,),
        in_specs=[qspec, kspec, kspec,
                  pl.BlockSpec((ra, 128), lambda p: (0, 0)), pl.BlockSpec((ra, 128), lambda p: (0, 0))]
        + [pl.BlockSpec(memory_space=pl.ANY)] * len(deps),
        out_specs=[qspec, pl.BlockSpec((1, 2, rq), lambda p: (p, 0, 0))],
        out_shape=[jax.ShapeDtypeStruct((rq, w), F32), jax.ShapeDtypeStruct((pairs, 2, rq), F32)],
        scratch_shapes=[pltpu.VMEM((2, rq, 256), BF), pltpu.VMEM((2, rk, 256), BF), pltpu.VMEM((2, 128, rk), BF)],
        compiler_params=pltpu.CompilerParams(vmem_limit_bytes=28 << 20),
        cost_estimate=pl.CostEstimate(flops=(int(2e10) if causal else int(4e9)) * pairs, bytes_accessed=rq * w * 16, transcendentals=0),
        name="attn_fwd",
    )(q, k, v, qaux, kaux, *deps)


def attn_bwd_kernel(q_ref, k_ref, v_ref, do_ref, l_ref, d_ref, qa_ref, ka_ref, *refs, causal, qb, kb, rq, rk):
    dq_ref, dk_ref, dv_ref, qs, ks, kt, vs, dos, dka, dva = refs[-10:]
    lane = lax.broadcasted_iota(jnp.int32, (256, 128), 1)
    left = lane < HEAD

    def sel(a, b):
        return jnp.where(left, a, b)

    def build_q(i, _):
        r = pl.ds(pl.multiple_of(i * 256, 256), 256)
        hi, lo = split(q_ref[r, :] * (HEAD ** -0.5 * LOG2E))
        hir, lor = pltpu.roll(hi, HEAD, 1), pltpu.roll(lo, HEAD, 1)
        aux = qa_ref[r, :].astype(F32) if causal else jnp.zeros((256, 128), F32)
        qs[0, r, 0:128] = sel(hi, lor).astype(BF)
        qs[0, r, 128:256] = sel(hi, aux).astype(BF)
        qs[1, r, 0:128] = sel(hir, lo).astype(BF)
        qs[1, r, 128:256] = sel(hir, aux).astype(BF)
        hi, lo = split(do_ref[r, :])
        hir, lor = pltpu.roll(hi, HEAD, 1), pltpu.roll(lo, HEAD, 1)
        zero = jnp.zeros((256, 128), F32)
        dos[0, r, 0:128] = sel(hi, lor).astype(BF)
        dos[0, r, 128:256] = sel(hi, zero).astype(BF)
        dos[1, r, 0:128] = sel(hir, lo).astype(BF)
        dos[1, r, 128:256] = sel(hir, zero).astype(BF)
        return 0

    def build_k(i, _):
        r = pl.ds(pl.multiple_of(i * 256, 256), 256)
        hi, lo = split(k_ref[r, :])
        hir, lor = pltpu.roll(hi, HEAD, 1), pltpu.roll(lo, HEAD, 1)
        aux = ka_ref[r, :].astype(F32) if causal else jnp.zeros((256, 128), F32)
        ks[0, r, 0:128] = sel(hi, hir).astype(BF)
        ks[0, r, 128:256] = sel(lo, aux).astype(BF)
        ks[1, r, 0:128] = sel(hir, hi).astype(BF)
        ks[1, r, 128:256] = sel(lor, aux).astype(BF)
        kt[0, :, r] = sel(hi, lor).T.astype(BF)
        kt[1, :, r] = sel(hir, lo).T.astype(BF)
        hi, lo = split(v_ref[r, :])
        hir, lor = pltpu.roll(hi, HEAD, 1), pltpu.roll(lo, HEAD, 1)
        zero = jnp.zeros((256, 128), F32)
        vs[0, r, 0:128] = sel(hi, hir).astype(BF)
        vs[0, r, 128:256] = sel(lo, zero).astype(BF)
        vs[1, r, 0:128] = sel(hir, hi).astype(BF)
        vs[1, r, 128:256] = sel(lor, zero).astype(BF)
        dka[0, r, :] = zero
        dka[1, r, :] = zero
        dva[0, r, :] = zero
        dva[1, r, :] = zero
        return 0

    lax.fori_loop(0, rq // 256, build_q, 0)
    lax.fori_loop(0, rk // 256, build_k, 0)

    def one_q(i, _):
        rows = pl.ds(pl.multiple_of(i * qb, qb), qb)

        def update(acc, h, keys, cols, mask):
            qh = qs[h, cols, :]
            dh = dos[h, cols, :]
            st = dot(ks[h, keys, :], qh, NT)
            if mask is not None:
                kk = lax.broadcasted_iota(jnp.int32, st.shape, 0)
                qq = lax.broadcasted_iota(jnp.int32, st.shape, 1)
                st = jnp.where(kk - qq <= mask, st, -1e30)
            p = jnp.exp2(st - l_ref[0, h:h + 1, cols])
            ph = p.astype(BF)
            plo = (p - ph.astype(F32)).astype(BF)
            dhl = dh[:, 0:128]
            dva[h, keys, :] += dot(ph, dhl) + dot(plo, dhl)
            dp = dot(vs[h, keys, :], dh, NT)
            ds = p * (dp - d_ref[0, h:h + 1, cols])
            dsh = ds.astype(BF)
            dsl = (ds - dsh.astype(F32)).astype(BF)
            qhl = qh[:, 0:128]
            dka[h, keys, :] += dot(dsh, qhl) + dot(dsl, qhl)
            kth = kt[h, :, keys]
            return acc + dot(kth, dsh) + dot(kth, dsl)

        def step(j, carry):
            keys = pl.ds(pl.multiple_of(j * kb, kb), kb)
            return tuple(update(carry[h], h, keys, rows, None) for h in range(2))

        init = jnp.zeros((128, qb), F32)
        carry = (init, init)
        if causal:
            carry = lax.fori_loop(0, i * qb // kb, step, carry)
            sub = qb // 2
            for j in range(2):
                keys = pl.ds(pl.multiple_of(i * qb + j * sub, sub), sub)
                cols = pl.ds(pl.multiple_of(i * qb + j * sub, sub), qb - j * sub)
                new = []
                for h in range(2):
                    part = update(carry[h][:, j * sub:], h, keys, cols, 0)
                    if j:
                        part = jnp.concatenate([carry[h][:, :sub], part], axis=1)
                    new.append(part)
                carry = tuple(new)
        else:
            for j in range(rk // kb):
                carry = step(j, carry)
        outs = [(a[0:HEAD] + a[HEAD:]) * (HEAD ** -0.5) for a in carry]
        dq_ref[rows, :] = jnp.concatenate(outs, axis=0).T
        return 0

    lax.fori_loop(0, rq // qb, one_q, 0)

    def finish(i, _):
        r = pl.ds(pl.multiple_of(i * 256, 256), 256)
        a, b = dka[0, r, :], dka[1, r, :]
        dk_ref[r, :] = sel(a + pltpu.roll(a, HEAD, 1), b + pltpu.roll(b, HEAD, 1)) * LN2
        a, b = dva[0, r, :], dva[1, r, :]
        dv_ref[r, :] = sel(a + pltpu.roll(a, HEAD, 1), b + pltpu.roll(b, HEAD, 1))
        return 0

    lax.fori_loop(0, rk // 256, finish, 0)


def attn_bwd(q, k, v, do, lse, delta, qaux, kaux, causal, qb=512, kb=512, pair=None, deps=(), prev=()):
    rq, w = q.shape
    rk = k.shape[0]
    pairs = 1 if pair is not None else w // 128
    first = pair or 0
    deps = list(prev) + list(deps)
    ra = qaux.shape[0]
    qspec = pl.BlockSpec((rq, 128), lambda p: (0, p + first))
    kspec = pl.BlockSpec((rk, 128), lambda p: (0, p + first))
    lspec = pl.BlockSpec((1, 2, rq), lambda p: (p + first, 0, 0))
    aspec = pl.BlockSpec((ra, 128), lambda p: (0, 0))
    return pl.pallas_call(
        functools.partial(attn_bwd_kernel, causal=causal, qb=qb, kb=kb, rq=rq, rk=rk),
        grid=(pairs,),
        in_specs=[qspec, kspec, kspec, qspec, lspec, lspec, aspec, aspec]
        + [pl.BlockSpec(memory_space=pl.ANY)] * len(deps),
        out_specs=[qspec, kspec, kspec],
        out_shape=[jax.ShapeDtypeStruct((n, w), F32) for n in (rq, rk, rk)],
        input_output_aliases={8 + i: i for i in range(len(prev))},
        scratch_shapes=[pltpu.VMEM((2, rq, 256), BF), pltpu.VMEM((2, rk, 256), BF), pltpu.VMEM((2, 128, rk), BF),
                        pltpu.VMEM((2, rk, 256), BF), pltpu.VMEM((2, rq, 256), BF),
                        pltpu.VMEM((2, rk, 128), F32), pltpu.VMEM((2, rk, 128), F32)],
        compiler_params=pltpu.CompilerParams(vmem_limit_bytes=40 << 20),
        cost_estimate=pl.CostEstimate(flops=(int(3.4e10) if causal else int(5e9)) * pairs, bytes_accessed=rq * w * 32, transcendentals=0),
        name="attn_bwd",
    )(q, k, v, do, lse, delta, qaux, kaux, *deps)


def attn_bwd_inputs_kernel(q_ref, k_ref, v_ref, do_ref, l_ref, d_ref, qa_ref, ka_ref, x_ref, wq_ref, wk_ref, wv_ref,
                           *refs, qb, kb, rq, rk, more):
    part_ref, g_ref, dq, dk, dv = refs[-12:-7]
    scratch = refs[-7:]
    attn_bwd_kernel(
        q_ref, k_ref, v_ref, do_ref, l_ref, d_ref, qa_ref, ka_ref, dq, dk, dv, *scratch,
        causal=True, qb=qb, kb=kb, rq=rq, rk=rk,
    )
    weights = parts2(jnp.concatenate([wq_ref[...], wk_ref[...], wv_ref[...]], axis=1))
    step = 512
    g_ref[...] = jnp.zeros(g_ref.shape, F32)

    def body(i, _):
        r = pl.ds(pl.multiple_of(i * step, step), step)
        grads = parts2(jnp.concatenate([dq[r, :], dk[r, :], dv[r, :]], axis=1))
        new = dot3(grads, weights, NT)
        part_ref[r, :] = new + refs[0][r, :] if more else new
        g_ref[...] += dot3(parts2(x_ref[r, :].T), grads)
        return 0

    lax.fori_loop(0, rq // step, body, 0)


def attn_bwd_inputs(q, k, v, do, lse, delta, qaux, kaux, x, weights, qb, kb, pair, prev=None, deps=()):
    rows, w = q.shape
    width = x.shape[1]
    one = pl.Buffered(1)
    qspec = pl.BlockSpec((rows, 128), lambda p: (0, pair), pipeline_mode=one)
    lspec = pl.BlockSpec((1, 2, rows), lambda p: (pair, 0, 0))
    aspec = pl.BlockSpec((rows, 128), lambda p: (0, 0), pipeline_mode=one)
    wspec = pl.BlockSpec((width, 128), lambda p: (0, pair), pipeline_mode=one)
    xspec = pl.BlockSpec((rows, width), lambda p: (0, 0), pipeline_mode=one)
    first = () if prev is None else (prev,)
    return pl.pallas_call(
        functools.partial(attn_bwd_inputs_kernel, qb=qb, kb=kb, rq=rows, rk=rows, more=bool(first)),
        grid=(1,),
        in_specs=[qspec] * 4 + [lspec, lspec, aspec, aspec, xspec, wspec, wspec, wspec] + [xspec] * len(first)
        + [pl.BlockSpec(memory_space=pl.ANY)] * len(deps),
        out_specs=[xspec, pl.BlockSpec((width, 384), lambda p: (0, 0), pipeline_mode=one)],
        out_shape=[jax.ShapeDtypeStruct((rows, width), F32), jax.ShapeDtypeStruct((width, 384), F32)],
        scratch_shapes=[pltpu.VMEM((rows, 128), F32)] * 3
        + [pltpu.VMEM((2, rows, 256), BF), pltpu.VMEM((2, rows, 256), BF), pltpu.VMEM((2, 128, rows), BF),
           pltpu.VMEM((2, rows, 256), BF), pltpu.VMEM((2, rows, 256), BF),
           pltpu.VMEM((2, rows, 128), F32), pltpu.VMEM((2, rows, 128), F32)],
        compiler_params=pltpu.CompilerParams(vmem_limit_bytes=48 << 20),
        cost_estimate=pl.CostEstimate(flops=int(4e10), bytes_accessed=rows * w * 32, transcendentals=0),
        name="attn_bwd_inputs",
    )(q, k, v, do, lse, delta, qaux, kaux, x, *weights, *first, *deps)


def tree_aux(lengths, parent, n):
    segs = lengths.shape[0]
    ends = jnp.cumsum(lengths)
    places = jnp.arange(n, dtype=jnp.int32)
    seg = jnp.sum((places[:, None] >= ends[None, :-1]).astype(jnp.int32), axis=1)
    labels = jnp.arange(segs, dtype=jnp.int32)
    onehot = seg[:, None] == labels[None, :]
    up1 = jnp.sum(jnp.where(onehot, parent[None, :], 0), axis=1)
    up2 = jnp.sum(jnp.where(up1[:, None] == labels[None, :], parent[None, :], 0), axis=1)
    lab = jnp.arange(128, dtype=jnp.int32)[None, :] - HEAD
    inside = (lab >= 0) & (lab < segs)
    sg = seg[:, None]
    kaux = jnp.where(inside & (lab == sg), 1.0, 0.0).astype(BF)
    ok = (lab == sg) | ((sg > 0) & ((lab == up1[:, None]) | (lab == up2[:, None])))
    qaux = jnp.where(inside & ~ok, -1e30, 0.0).astype(BF)
    return qaux, kaux


HIGH = lax.Precision.HIGH
TN = (((0,), (0,)), ((), ()))
BOTH = ("dp", "tensor")
ANY = pl.BlockSpec(memory_space=pl.ANY)
VMEM = pl.BlockSpec(memory_space=pltpu.VMEM)
SMEM = pl.BlockSpec(memory_space=pltpu.SMEM)


def mm(a, b, dims=NN):
    return lax.dot_general(a, b, dims, precision=HIGH, preferred_element_type=F32)


def nothing(*refs):
    pass


def corner(x):
    return x if x.ndim < 2 else x.reshape((-1,) + x.shape[-1:])[:8, :128]


def after(x, *others):
    return pl.pallas_call(
        nothing,
        in_specs=[ANY] * (1 + len(others)),
        out_specs=ANY,
        out_shape=jax.ShapeDtypeStruct(x.shape, x.dtype),
        input_output_aliases={0: 0},
        name="after",
    )(x, *others)


def flip_bit(size, bit):
    return [(i, i ^ (1 << bit)) for i in range(size)]


def turn(size, by):
    return [(i, (i + by) % size) for i in range(size)]


def pick(x, axis, index):
    return lax.dynamic_index_in_dim(x, index, axis, keepdims=False)


def item_routes(dp, tensor):
    routes = []
    for step in range(2):
        pairs = []
        for c in range(dp // 2):
            for t in range(2):
                for z in range(tensor):
                    b = (z + step) % 2
                    pairs.append(((2 * c + t) * tensor + z, (2 * c + z // 2) * tensor + 2 * b + t))
        routes.append(pairs)
    return routes


def send_items(x, routes, z, *others):
    first, second = pick(x, 0, z % 2), pick(x, 0, 1 - z % 2)
    if others:
        first, second = after(first, *others), after(second, *others)
    return lax.ppermute(first, BOTH, routes[0]), lax.ppermute(second, BOTH, routes[1])


def in_order(first, second, z):
    return jnp.where(z // 2 == 0, jnp.concatenate([first, second]), jnp.concatenate([second, first]))


def return_items(rows, routes, z, between=None):
    half = rows.shape[0] // 2
    b = z // 2
    back = [[(t, s) for s, t in r] for r in routes]
    first = lax.ppermute(lax.dynamic_slice_in_dim(rows, b * half, half), BOTH, back[0])
    second = lax.dynamic_slice_in_dim(rows, (1 - b) * half, half)
    if between is not None:
        second = after(second, first, between)
    return first, lax.ppermute(second, BOTH, back[1])


def both_batches(first, second, z):
    return jnp.where(z % 2 == 0, jnp.stack([first, second]), jnp.stack([second, first]))


def swap(x, dp):
    return lax.ppermute(x, "dp", flip_bit(dp, 0))


def both_cores(mine, other, k, axis=0):
    return jnp.where(
        k == 0, jnp.concatenate([mine, other], axis), jnp.concatenate([other, mine], axis)
    )


def rows_kernel(who_ref, a_ref, b_ref, c_ref, d_ref, o_ref):
    k, m = who_ref[0], who_ref[1]
    half = a_ref.shape[0]
    for ref, core, which in ((a_ref, k, m), (b_ref, k, 1 - m), (c_ref, 1 - k, m), (d_ref, 1 - k, 1 - m)):
        o_ref[pl.ds(pl.multiple_of((2 * core + which) * half, half), half), :] = ref[...]


def place_rows(first, second, other_first, other_second, k, z):
    half, width = first.shape
    who = jnp.stack([k, z // 2]).astype(jnp.int32)
    return pl.pallas_call(
        rows_kernel,
        in_specs=[SMEM, VMEM, VMEM, VMEM, VMEM],
        out_specs=VMEM,
        out_shape=jax.ShapeDtypeStruct((4 * half, width), F32),
        compiler_params=pltpu.CompilerParams(vmem_limit_bytes=32 << 20),
        cost_estimate=pl.CostEstimate(flops=0, bytes_accessed=32 * half * width, transcendentals=0),
        name="place_rows",
    )(who, first, second, other_first, other_second)


ROOT_HALF = 0.7071067811865476
NORMAL_PEAK = 0.3989422804014327


def parts2(x):
    hi = x.astype(BF)
    return hi, (x - hi.astype(F32)).astype(BF)


def dot3(a, b, dims=NN):
    return dot(a[0], b[0], dims) + (dot(a[0], b[1], dims) + dot(a[1], b[0], dims))


def ffn_kernel(z_ref, h_ref, g_ref, wi_ref, wo_ref, bo_ref, out_ref, dh_ref, gr_ref, bi_ref, go_ref,
               hh, hl, gh, gl, hth, htl, gth, gtl, ah, al, dh, dl, *, rb, drows):
    j = pl.program_id(0)
    n = h_ref.shape[0]

    @pl.when(j == 0)
    def _():
        for r in range(n // rb):
            rows = slice(r * rb, (r + 1) * rb)
            for ref, h, l, th, tl in ((h_ref, hh, hl, hth, htl), (g_ref, gh, gl, gth, gtl)):
                x = ref[rows, :]
                h[rows, :], l[rows, :] = parts2(x)
                th[:, rows], tl[:, rows] = parts2(x.T)
            out_ref[rows, :] = h_ref[rows, :] + bo_ref[0:1, :]
            dh_ref[rows, :] = g_ref[rows, :]

    dp = wi_ref.shape[0]
    wide = wi_ref.shape[3]
    wi = parts2(wi_ref[:, 0, 0:drows, :].reshape(dp * drows, wide))
    wo = parts2(wo_ref[:, 0, 0:drows, :].reshape(dp * drows, wide))
    bias = wi_ref[0, 0, drows:drows + 1, :]
    total = jnp.zeros((1, wide), F32)
    for r in range(n // rb):
        rows = slice(r * rb, (r + 1) * rb)
        u = dot3((hh[rows, :], hl[rows, :]), wi) + bias
        gz = dot3((gh[rows, :], gl[rows, :]), wo)
        cdf = 0.5 * (1.0 + lax.erf(u * ROOT_HALF))
        act = u * cdf
        du = gz * (cdf + u * (NORMAL_PEAK * jnp.exp(-0.5 * u * u)))
        total = total + jnp.sum(du, axis=0, keepdims=True)
        act, du = parts2(act), parts2(du)
        ah[rows, :], al[rows, :] = act
        dh[rows, :], dl[rows, :] = du
        out_ref[rows, :] += dot3(act, wo, NT)
        dh_ref[rows, :] += dot3(du, wi, NT)
    gr_ref[:, :, 0:wide] = dot3((hth[...], htl[...]), (dh[...], dl[...])).reshape(dp, drows, wide)
    gr_ref[:, :, wide:] = dot3((gth[...], gtl[...]), (ah[...], al[...])).reshape(dp, drows, wide)
    bi_ref[0:1, :] = total

    @pl.when(j == 0)
    def _():
        go_ref[0:1, :] = jnp.sum(g_ref[...], axis=0, keepdims=True)


def ffn(h2, g, ff_all, bias_out, z, drows):
    n, width = h2.shape
    dp, tensor, high, both = ff_all.shape
    wide = both // 4
    steps = 2 * tensor
    full = lambda: pl.BlockSpec((n, width), lambda j, z: (0, 0))
    return pl.pallas_call(
        functools.partial(ffn_kernel, rb=512, drows=drows),
        grid_spec=pltpu.PrefetchScalarGridSpec(
            num_scalar_prefetch=1,
            grid=(steps,),
            in_specs=[
                full(), full(),
                pl.BlockSpec((dp, 1, high, wide), lambda j, z: (0, (z[0] + tensor - j // 2) % tensor, 0, j % 2)),
                pl.BlockSpec((dp, 1, high, wide), lambda j, z: (0, (z[0] + tensor - j // 2) % tensor, 0, 2 + j % 2)),
                pl.BlockSpec((1, width), lambda j, z: (0, 0)),
            ],
            out_specs=[
                full(), full(), pl.BlockSpec((dp, drows, 2 * wide), lambda j, z: (0, 0, j)),
                pl.BlockSpec((1, wide), lambda j, z: (0, j)), pl.BlockSpec((1, width), lambda j, z: (0, 0)),
            ],
            scratch_shapes=[pltpu.VMEM((n, width), BF)] * 4 + [pltpu.VMEM((width, n), BF)] * 4
            + [pltpu.VMEM((n, wide), BF)] * 4,
        ),
        out_shape=[
            jax.ShapeDtypeStruct((n, width), F32),
            jax.ShapeDtypeStruct((n, width), F32),
            jax.ShapeDtypeStruct((dp, drows, 2 * wide * steps), F32),
            jax.ShapeDtypeStruct((1, wide * steps), F32),
            jax.ShapeDtypeStruct((1, width), F32),
        ],
        compiler_params=pltpu.CompilerParams(vmem_limit_bytes=48 << 20),
        cost_estimate=pl.CostEstimate(flops=int(5e10), bytes_accessed=30 << 20, transcendentals=0),
        name="ffn",
    )(z[None].astype(jnp.int32), h2, g, ff_all, ff_all, bias_out[None])


def around(x, tensor):
    return [x] + [lax.ppermute(x, "tensor", turn(tensor, s)) for s in range(1, tensor)]


def place_kernel(who_ref, g_ref, *outs, widths, own):
    k, z = who_ref[0], who_ref[1]
    tensor = g_ref.shape[1]
    half = tensor // 2
    for s in range(tensor):
        col = (z + tensor - s) % tensor
        start = 0
        for o, w, only in zip(outs, widths, own):
            def copy(c, o=o, w=w, s=s, start=start):
                o[:, pl.ds(pl.multiple_of(c * w, w), w)] = g_ref[0, s, :, start:start + w]

            if only:
                pl.when(col // half == k)(functools.partial(copy, col % half))
            else:
                copy(col)
            start += w


def place_weights(g, widths, own, k, z):
    dp, tensor, rows, wide = g.shape
    who = jnp.stack([k, z]).astype(jnp.int32)
    cols = [w * (tensor // 2 if o else tensor) for o, w in zip(own, widths)]
    return pl.pallas_call(
        functools.partial(place_kernel, widths=widths, own=own),
        grid=(dp,),
        in_specs=[SMEM, pl.BlockSpec((1, tensor, rows, wide), lambda i: (i, 0, 0, 0))],
        out_specs=[pl.BlockSpec((rows, c), lambda i: (i, 0)) for c in cols],
        out_shape=[jax.ShapeDtypeStruct((dp * rows, c), F32) for c in cols],
        cost_estimate=pl.CostEstimate(flops=0, bytes_accessed=8 * dp * tensor * rows * wide, transcendentals=0),
        name="place_weights",
    )(who, g)


def halve(cur, seq, dp, d):
    left = sorted(seq, reverse=True)
    cur = cur.reshape((2,) * len(left) + cur.shape[1:])
    for bit in seq:
        axis = left.index(bit)
        mine = (d >> bit) & 1
        sent = lax.ppermute(pick(cur, axis, 1 - mine), "dp", flip_bit(dp, bit))
        cur = pick(cur, axis, mine) + sent
        left.remove(bit)
    return cur


def along_z(parts, tensor, z, *others):
    total = parts(z)
    for s in range(1, tensor):
        part = parts((z + s) % tensor)
        if others:
            part = after(part, *others)
        total = total + lax.ppermute(part, "tensor", turn(tensor, s))
    return total


def column_block(x, i, tensor):
    w = x.shape[-1] // tensor
    return lax.dynamic_slice_in_dim(x, i * w, w, x.ndim - 1)


def reduce_over_dp(mats, extra, dp, *others):
    whole = jnp.concatenate([m.reshape(dp, m.shape[0] // dp, m.shape[1]) for m in mats], axis=2)
    whole = jnp.concatenate([whole, jnp.broadcast_to(extra[None], (dp,) + extra.shape)], axis=1)
    return lax.psum_scatter(after(whole, *others), "dp", scatter_dimension=0, tiled=False)


def reduce_head_grads(mats, dp, tensor, d, z):
    bits = dp.bit_length() - 1
    k = d % 2
    chains = []
    for u, m in enumerate(mats):
        seq = list(range(1, bits))
        if u % 2:
            seq = seq[::-1]
        m = m.reshape(dp // 2, 2, m.shape[0] // dp, m.shape[1])
        both = jnp.stack([pick(m, 1, k), swap(pick(m, 1, 1 - k), dp)], axis=1)
        chains.append(halve(both, seq, dp, d))
    return jnp.stack(chains)


def on_device(
    inputs, memory, lengths, parent, self_qkv, self_out, cross_q, cross_kv, cross_out,
    ff_in, ff_bias_in, ff_out, ff_bias_out, cotangent,
):
    dp, tensor = lax.axis_size("dp"), lax.axis_size("tensor")
    d, z = lax.axis_index("dp"), lax.axis_index("tensor")
    k = d % 2
    routes = item_routes(dp, tensor)
    rows = inputs.shape[2] * 2
    width = inputs.shape[3]
    heads_wide = width // 2
    hw = self_qkv.shape[2]
    fw = ff_in.shape[1]
    drows = ff_in.shape[0]

    shard = jnp.concatenate(
        [self_qkv[0], self_qkv[1], self_qkv[2], self_out.T, cross_q, cross_kv[0], cross_kv[1], cross_out.T], axis=1
    )
    x_first, x_second = pick(inputs[:, 0], 0, z % 2), pick(inputs[:, 0], 0, 1 - z % 2)
    g_first, g_second = pick(cotangent[:, 0], 0, z % 2), pick(cotangent[:, 0], 0, 1 - z % 2)
    paths = jnp.concatenate([lengths[:, 0], parent[:, 0]], axis=1)
    other_paths = swap(paths, dp)
    m1, m2 = send_items(memory[:, 0], routes, z)
    parts = around(after(shard, x_first, x_second), tensor)
    weights = lax.all_gather(after(jnp.stack(parts), m1, m2, other_paths), "dp", axis=0)
    x1 = lax.ppermute(after(x_first, *parts[1:]), BOTH, routes[0])
    x2 = lax.ppermute(after(x_second, *parts[1:]), BOTH, routes[1])
    mem = in_order(m1, m2, z)
    mem_all = both_cores(mem, swap(mem, dp), k)

    my_path = pick(jnp.where(z % 2 == k, paths, other_paths), 0, z // 2)
    segs = lengths.shape[2]
    qaux, kaux = tree_aux(my_path[:segs], my_path[segs:], 2 * rows)

    bias_rows = jnp.concatenate([ff_bias_in[None], jnp.zeros((7, fw), F32)])
    ff_shard = jnp.concatenate(
        [jnp.concatenate([ff_in, ff_out.T], axis=1), jnp.concatenate([bias_rows] * 2, axis=1)]
    )
    ff_parts = around(after(ff_shard, x1, x2, mem_all, qaux, kaux, corner(g_first), corner(g_second)), tensor)
    wq, wk, wv, out_t, cq, ck, cv, cross_out_t = place_weights(
        weights, [hw] * 8, [True] * 3 + [False] * 5, k, z
    )
    own_w = [wq, wk, wv]
    x_all = place_rows(x1, x2, swap(x1, dp), swap(x2, dp), k, z)
    x = lax.dynamic_slice_in_dim(x_all, k * rows, rows)
    q, key, val = (mm(x_all, w) for w in own_w)
    ff_z = jnp.stack([ff_parts[0]] + [after(t, corner(q), corner(key), corner(val)) for t in ff_parts[1:]])
    ff_all = lax.all_gather(ff_z, "dp", axis=0)
    g1 = lax.ppermute(after(g_first, ff_z), BOTH, routes[0])
    g2 = lax.ppermute(after(g_second, ff_z), BOTH, routes[1])

    attn, lse = attn_fwd(q, key, val, qaux, kaux, True, 1024, 1024, deps=(ff_z,))
    mine = lax.dynamic_slice_in_dim(attn, k * rows, rows)
    other = swap(lax.dynamic_slice_in_dim(attn, (1 - k) * rows, rows), dp)
    attn_rows = both_cores(mine, other, k, 1)

    h1 = x + mm(attn_rows, out_t, NT)
    q2 = mm(h1, cq)
    k2, v2 = mm(mem_all, ck), mm(mem_all, cv)
    ctx, lse2 = attn_fwd(q2, k2, v2, qaux, kaux, False, 1024, 256)
    h2 = h1 + mm(ctx, cross_out_t, NT)
    g = in_order(g1, g2, z)
    output, dh2, ff_grads, du_sum, g_sum = ffn(h2, g, ff_all, ff_bias_out, z, drows)
    ff_mine = lax.psum_scatter(ff_grads, "dp", scatter_dimension=0, tiled=False)
    cut = fw // hw
    spare = jnp.zeros((1, (5 - cut) * tensor * hw), F32)
    bias_rows = jnp.concatenate([
        jnp.concatenate([du_sum.reshape(tensor, cut, hw).transpose(1, 0, 2).reshape(1, -1), spare], axis=1),
        jnp.concatenate([jnp.repeat(g_sum.reshape(cut, 1, hw), tensor, axis=1).reshape(1, -1), spare], axis=1),
        jnp.zeros((6, 5 * tensor * hw), F32),
    ])
    dctx = mm(dh2, cross_out_t)
    grad_cross_out_t = mm(dh2, ctx, TN)
    heads = width // HEAD
    pick_heads = (jnp.arange(width)[None, :] // HEAD == jnp.arange(heads)[:, None]).astype(F32)

    def deltas(a, b):
        prod = a * b
        n = prod.shape[1] // HEAD
        return lax.dot_general(
            pick_heads[:n, :prod.shape[1]], prod, NT, precision=lax.Precision.HIGHEST
        ).reshape(n // 2, 2, prod.shape[0])

    dq2, dk2, dv2 = attn_bwd(q2, k2, v2, dctx, lse2, deltas(dctx, ctx), qaux, kaux, False, 1024, 256)
    grad_cross_q = mm(h1, dq2, TN)
    grad_ck, grad_cv = mm(mem_all, dk2, TN), mm(mem_all, dv2, TN)
    mem_part = mm(dk2, ck, NT) + mm(dv2, cv, NT)
    mem_rows = mem_part.shape[0] // 2
    grad_mem = lax.dynamic_slice_in_dim(mem_part, k * mem_rows, mem_rows) + swap(
        lax.dynamic_slice_in_dim(mem_part, (1 - k) * mem_rows, mem_rows), dp
    )
    dh1 = dh2 + mm(dq2, cq, NT)
    dattn_rows = mm(dh1, out_t)
    grad_self_out_t = mm(dh1, attn_rows, TN)
    mine = lax.dynamic_slice_in_dim(dattn_rows, k * heads_wide, heads_wide, 1)
    other = swap(lax.dynamic_slice_in_dim(dattn_rows, (1 - k) * heads_wide, heads_wide, 1), dp)
    dattn = both_cores(mine, other, k)
    mid_mine = reduce_over_dp(
        [grad_cross_q, grad_ck, grad_cv, grad_cross_out_t, grad_self_out_t], bias_rows, dp, ff_mine
    )
    ff_sum = along_z(lambda i: column_block(ff_mine, i, tensor), tensor, z)
    out_back = return_items(output, routes, z)
    delta = deltas(dattn, attn)
    part, head_grads = None, []
    for p in range(heads_wide // 128):
        deps = [ff_mine]
        if p:
            ff_sum, *out_back = (after(t, corner(part)) for t in [ff_sum, *out_back])
            deps = [corner(t) for t in [ff_sum, *out_back]]
        part, got = attn_bwd_inputs(
            q, key, val, dattn, lse, delta, qaux, kaux, x_all, own_w, 1024, 512, p, prev=part, deps=deps
        )
        head_grads.append(got)
    dx = (
        dh1
        + lax.dynamic_slice_in_dim(part, k * rows, rows)
        + swap(lax.dynamic_slice_in_dim(part, (1 - k) * rows, rows), dp)
    )
    def mid_parts(i):
        return jnp.concatenate(
            [column_block(mid_mine[:, n * width:(n + 1) * width], i, tensor) for n in range(5)], axis=1
        )

    mid_sum = along_z(mid_parts, tensor, z, corner(dx))
    x_back = return_items(dx, routes, z, between=corner(mid_sum))
    head_grads = [after(t, corner(mid_sum)) for t in head_grads]
    mem_back = return_items(after(grad_mem, corner(mid_sum)), routes, z)
    ff_sum = ff_sum.reshape(drows, 2, 2, fw // 2)
    grad_ff_in = ff_sum[:, :, 0].reshape(drows, fw)
    grad_ff_out = ff_sum[:, :, 1].reshape(drows, fw)

    mid = [mid_sum[:drows, n * hw:(n + 1) * hw] for n in range(5)]
    grad_bias_in, grad_bias_out = mid_sum[drows, :fw], mid_sum[drows + 1, :fw]
    head_sums = reduce_head_grads(head_grads, dp, tensor, d, z)
    half = tensor // 2
    att = along_z(
        lambda i: pick(pick(head_sums, 0, i % half), 0, (i // half + k) % 2), tensor, z,
    )
    att = [att[:, n * hw:(n + 1) * hw] for n in range(3)]
    return (
        both_batches(*out_back, z)[:, None],
        both_batches(*x_back, z)[:, None],
        both_batches(*mem_back, z)[:, None],
        jnp.stack(att),
        mid[4].T,
        mid[0],
        jnp.stack(mid[1:3]),
        mid[3].T,
        grad_ff_in,
        grad_bias_in,
        grad_ff_out.T,
        grad_bias_out,
    )


def solution(mesh):
    rows4 = P(None, "dp", "tensor", None)
    col3, row2, col2 = P(None, "dp", "tensor"), P("tensor", "dp"), P("dp", "tensor")
    idx = P(None, "dp", None)
    return jax.shard_map(
        on_device,
        mesh=mesh,
        in_specs=(rows4, rows4, idx, idx, col3, row2, col2, col3, row2, col2, P("tensor"), row2, P(), rows4),
        out_specs=(rows4, rows4, rows4, col3, row2, col2, col3, row2, col2, P("tensor"), row2, P()),
        check_vma=False,
    )
```
